512 devices in a mesh: azim: 32 (over y, x), axial: 8 (over z_lo, core), radial: 2 (over z_hi).
Axes of the slice: x: 4, y: 8, z: 8 (z_hi: 2, z_lo: 4; z = z_hi * 4 + z_lo), core: 2. Of those that a mesh axis runs over, the one named last changes fastest.
Arguments:
- density: float32 [128, 64, 256], P('azim', 'axial', 'radial'), may hold values from 0.9 to 1.1
- momentum: float32 [3, 128, 64, 256], P(None, 'azim', 'axial', 'radial'), may hold values from -0.35 to 0.35
- energy: float32 [128, 64, 256], P('azim', 'axial', 'radial'), may hold values from 1.5 to 2.21, as said below
- wall_flags: int32 [32, 16], P('azim', 'axial'), may hold values 0 or 1
- body_motion: float32 [6], replicated, may hold values from -0.15 to 0.15
Outputs:
- density_change: float32 [128, 64, 256], P('azim', 'axial', 'radial')
- momentum_change: float32 [3, 128, 64, 256], P(None, 'azim', 'axial', 'radial')
- energy_change: float32 [128, 64, 256], P('azim', 'axial', 'radial')
- body_next: float32 [6], replicated
The draws below stay inside these ranges and needn't reach their ends.
Inputs may be any that keep to these rules, and one draw needn't show every extreme that they name: At every point energy minus |momentum|^2 / (2 density) lies between 1.5 and 2.0.
All inputs are finite; a program needn't handle non-finite values. No bound on the sum of `wall_flags` on one device may be relied on, other than what follows from the above.
Results may differ from the reference program's by a relative error of at most 0.0003.
Values sent between devices are 32-bit elements; how exact they have to be, the bound alone decides.
A program may use at most 64 MiB of HBM per device.

```python
import math
import jax
import jax.numpy as jnp
import numpy as np
from jax import lax

AZIM_TOTAL = 32
AXIAL_TOTAL = 16
RADIAL_TOTAL = 64
AZIM_NODES = 128
AXIAL_NODES = 64
RADIAL_NODES = 256


def flow_fields(key, exponent):
    key_dens, key_mom, key_press = jax.random.split(key, 3)
    grid_shape = (AZIM_NODES, AXIAL_NODES, RADIAL_NODES)
    density = 0.9 + 0.2 * jax.random.uniform(key_dens, grid_shape, jnp.float32) ** exponent
    momentum = 0.35 * jax.random.uniform(key_mom, (3,) + grid_shape, jnp.float32, -1.0, 1.0)
    rough = jax.random.uniform(key_press, grid_shape, jnp.float32)
    pressure = 0.6 + 0.2 * rough
    kinetic = momentum[0] * momentum[0] + momentum[1] * momentum[1] + momentum[2] * momentum[2]
    energy = pressure / 0.4 + 0.5 * kinetic / density
    return (density, momentum, energy)


def draw_density(key, part):
    fields = flow_fields(key, 1.0)
    return fields[0]


def draw_momentum(key, part):
    fields = flow_fields(key, 1.0)
    return fields[1]


def draw_energy(key, part):
    fields = flow_fields(key, 1.0)
    return fields[2]


def plant(drawn, own_key, low, high):
    dims = drawn.shape
    place = [jax.random.randint(jax.random.fold_in(own_key, axis), (), 0, dims[axis]) for axis in range(len(dims))]
    drawn = drawn.at[tuple(place)].set(low)
    longest = dims.index(max(dims))
    place[longest] = (place[longest] + 1) % dims[longest]
    return drawn.at[tuple(place)].set(high)


def setup_inputs(seed: int = 0) -> dict:
    seeds = jax.random.split(jax.random.key(seed), 6)
    return {
        "density": draw_density(jax.random.fold_in(seeds[5], 71), 0),
        "momentum": draw_momentum(jax.random.fold_in(seeds[5], 71), 0),
        "energy": draw_energy(jax.random.fold_in(seeds[5], 71), 0),
        "wall_flags": plant((jax.random.randint(seeds[3], (AZIM_TOTAL, AXIAL_TOTAL), 0, 4) < 3).astype(jnp.int32), jax.random.fold_in(seeds[3], 1), 0, 1),
        "body_motion": jnp.clip(jax.random.uniform(seeds[4], (6,), jnp.float32, -0.15, 0.15), -0.15, 0.15),
    }


heat_ratio = 1.4
radius_in = 1.0
radius_out = 3.0
store_length = 8.0
cfl_number = 0.05
body_gain = 30.0
body_mass = 0.5
inertia_diag = (1.0, 1.0, 0.25)
free_values = (1.0, 0.0, 0.0, 0.5, 1.0 / (1.4 * 0.4) + 0.125)
highest = lax.Precision.HIGHEST

def fr_tables():
    outer_point = np.sqrt(3.0 / 7.0 + 2.0 / 7.0 * np.sqrt(6.0 / 5.0))
    inner_point = np.sqrt(3.0 / 7.0 - 2.0 / 7.0 * np.sqrt(6.0 / 5.0))
    points = np.array([-outer_point, -inner_point, inner_point, outer_point])
    outer_weight = (18.0 - np.sqrt(30.0)) / 36.0
    inner_weight = (18.0 + np.sqrt(30.0)) / 36.0
    weights = np.array([outer_weight, inner_weight, inner_weight, outer_weight])
    bary_weights = np.array([1.0 / np.prod([points[i] - points[j] for j in range(4) if j != i]) for i in range(4)])
    derivative = np.zeros((4, 4))
    for i in range(4):
        for j in range(4):
            if i != j:
                derivative[i, j] = bary_weights[j] / bary_weights[i] / (points[i] - points[j])
        derivative[i, i] = -np.sum(derivative[i])

    def basis_at(location):
        return np.array([np.prod([(location - points[j]) / (points[i] - points[j]) for j in range(4) if j != i]) for i in range(4)])
    at_lower = basis_at(-1.0)
    at_upper = basis_at(1.0)
    third_slope = 0.5 * (15.0 * points * points - 3.0)
    fourth_slope = 0.5 * (35.0 * points ** 3 - 15.0 * points)
    slope_left = 0.5 * (fourth_slope - third_slope)
    slope_right = 0.5 * (fourth_slope + third_slope)
    return (points, weights, derivative, at_lower, at_upper, slope_left, slope_right)

def coordinates(node_count, first_elem, spacing, points):
    element_count = node_count // 4
    offsets = jnp.tile(jnp.asarray((points + 1.0) / 2.0, jnp.float32), element_count)
    element = (first_elem + jnp.arange(node_count, dtype=jnp.int32) // 4).astype(jnp.float32)
    return ((element + offsets) * spacing, element * spacing, (element + 1.0) * spacing)

def pressure_of(conserved):
    kinetic = conserved[1] * conserved[1] + conserved[2] * conserved[2] + conserved[3] * conserved[3]
    return (heat_ratio - 1.0) * (conserved[4] - 0.5 * kinetic / conserved[0])

def normal_velocity(conserved, normal):
    return (conserved[1] * normal[0] + conserved[2] * normal[1] + conserved[3] * normal[2]) / conserved[0]

def normal_flux(conserved, normal, grid_speed):
    pressure = pressure_of(conserved)
    vel_normal = normal_velocity(conserved, normal)
    relative = vel_normal - grid_speed
    return jnp.stack([conserved[0] * relative, conserved[1] * relative + pressure * normal[0], conserved[2] * relative + pressure * normal[1], conserved[3] * relative + pressure * normal[2], conserved[4] * relative + pressure * vel_normal])

def line_speed(conserved, normal):
    sound = jnp.sqrt(heat_ratio * pressure_of(conserved) / conserved[0])
    return jnp.abs(normal_velocity(conserved, normal)) + sound

def rusanov(minus_side, plus_side, speed_minus, speed_plus, normal, grid_speed, metric):
    wave_bound = jnp.maximum(speed_minus, speed_plus) + jnp.abs(grid_speed)
    average = 0.5 * (normal_flux(minus_side, normal, grid_speed) + normal_flux(plus_side, normal, grid_speed))
    return metric * (average - 0.5 * wave_bound * (plus_side - minus_side))

def wall_flux(plus_side, normal, grid_speed, metric):
    pressure = pressure_of(plus_side)
    zero_part = jnp.zeros_like(pressure)
    return metric * jnp.stack([zero_part, pressure * normal[0], pressure * normal[1], pressure * normal[2], pressure * grid_speed])

def free_speed(normal_z):
    return 0.5 * jnp.abs(normal_z) + 1.0

def free_state(target_shape):
    free_base = jnp.asarray(free_values, jnp.float32).reshape((5,) + (1,) * (len(target_shape) - 1))
    return jnp.broadcast_to(free_base, target_shape)

def radial_grid(motion, angle_pos, axial_pos):
    cos_t = jnp.cos(angle_pos)
    sin_t = jnp.sin(angle_pos)
    return motion[0] * cos_t + motion[1] * sin_t + axial_pos * (motion[4] * cos_t - motion[3] * sin_t)

def azim_grid(motion, angle_pos, axial_pos, radius):
    cos_t = jnp.cos(angle_pos)
    sin_t = jnp.sin(angle_pos)
    return -motion[0] * sin_t + motion[1] * cos_t + motion[5] * radius - axial_pos * (motion[4] * sin_t + motion[3] * cos_t)

def axial_grid(motion, angle_pos, radius):
    return motion[2] + radius * (motion[3] * jnp.sin(angle_pos) - motion[4] * jnp.cos(angle_pos))

def rigid_update(motion, wall_loads):
    velocity = motion[:3]
    rates_now = motion[3:]
    inertia = jnp.asarray(inertia_diag, jnp.float32)
    ang_momentum = inertia * rates_now
    gyroscopic = jnp.stack([rates_now[1] * ang_momentum[2] - rates_now[2] * ang_momentum[1], rates_now[2] * ang_momentum[0] - rates_now[0] * ang_momentum[2], rates_now[0] * ang_momentum[1] - rates_now[1] * ang_momentum[0]])
    zero_part = jnp.zeros_like(wall_loads[0])
    force_vec = jnp.stack([wall_loads[0], wall_loads[1], zero_part])
    torque = jnp.stack([wall_loads[2], wall_loads[3], zero_part])
    return jnp.concatenate([velocity + body_gain * force_vec / body_mass, rates_now + body_gain * (torque - gyroscopic) / inertia])

def frame_source(conserved, rates):
    zero_part = jnp.zeros_like(conserved[0])
    return jnp.stack([zero_part, -(rates[1] * conserved[3] - rates[2] * conserved[2]), -(rates[2] * conserved[1] - rates[0] * conserved[3]), -(rates[0] * conserved[2] - rates[1] * conserved[1]), zero_part])

def line_traces(conserved, normal, tables):
    at_lower = jnp.asarray(tables[3], jnp.float32)
    at_upper = jnp.asarray(tables[4], jnp.float32)
    half_weights = jnp.asarray(0.5 * tables[1], jnp.float32)
    lower_trace = jnp.einsum('...k,k->...', conserved, at_lower, precision=highest)
    upper_trace = jnp.einsum('...k,k->...', conserved, at_upper, precision=highest)
    speed_mean = jnp.einsum('...k,k->...', line_speed(conserved, normal), half_weights, precision=highest)
    return (lower_trace, upper_trace, speed_mean)

def face_slice(member, begin_at, end_at):
    if isinstance(member, float) or member.shape[-1] == 1:
        return member
    return member[..., begin_at:end_at]

def face_geometry(geometry, begin_at, end_at):
    normal, grid_speed, metric = geometry
    return (tuple((face_slice(member, begin_at, end_at) for member in normal)), face_slice(grid_speed, begin_at, end_at), face_slice(metric, begin_at, end_at))

def line_residual(conserved, node_geo, face_geo, low_side, high_side, tables):
    normal, grid_speed, metric = node_geo
    derivative = jnp.asarray(tables[2], jnp.float32)
    at_lower = jnp.asarray(tables[3], jnp.float32)
    at_upper = jnp.asarray(tables[4], jnp.float32)
    slope_left = jnp.asarray(tables[5], jnp.float32)
    slope_right = jnp.asarray(tables[6], jnp.float32)
    node_flux = metric * normal_flux(conserved, normal, grid_speed)
    lower_trace, upper_trace, speed_mean = line_traces(conserved, normal, tables)
    flux_diff = jnp.einsum('...k,jk->...j', node_flux, derivative, precision=highest)
    flux_lower = jnp.einsum('...k,k->...', node_flux, at_lower, precision=highest)
    flux_upper = jnp.einsum('...k,k->...', node_flux, at_upper, precision=highest)
    elem_count = conserved.shape[-2]
    inner_geo = face_geometry(face_geo, 1, elem_count)
    hat_inner = rusanov(upper_trace[..., :-1], lower_trace[..., 1:], speed_mean[..., :-1], speed_mean[..., 1:], inner_geo[0], inner_geo[1], inner_geo[2])
    first_geo = face_geometry(face_geo, 0, 1)
    if low_side is None:
        hat_first = wall_flux(lower_trace[..., :1], first_geo[0], first_geo[1], first_geo[2])
    else:
        hat_first = rusanov(low_side[0], lower_trace[..., :1], low_side[1], speed_mean[..., :1], first_geo[0], first_geo[1], first_geo[2])
    last_geo = face_geometry(face_geo, elem_count, elem_count + 1)
    hat_last = rusanov(upper_trace[..., -1:], high_side[0], speed_mean[..., -1:], high_side[1], last_geo[0], last_geo[1], last_geo[2])
    face_hats = jnp.concatenate([hat_first, hat_inner, hat_last], axis=-1)
    return flux_diff + slope_left * (face_hats[..., :-1, None] - flux_lower[..., None]) + slope_right * (face_hats[..., 1:, None] - flux_upper[..., None])

def reference(density, momentum, energy, wall_flags, body_motion):
    tables = fr_tables()
    at_lower = jnp.asarray(tables[3], jnp.float32)
    weights = jnp.asarray(tables[1], jnp.float32)
    step_azim = 2.0 * math.pi / AZIM_TOTAL
    step_axial = store_length / AXIAL_TOTAL
    step_radial = (radius_out - radius_in) / RADIAL_TOTAL
    time_step = cfl_number * min(step_radial, step_axial, radius_in * step_azim)
    angle_node = coordinates(AZIM_NODES, 0, step_azim, tables[0])[0]
    axial_node = coordinates(AXIAL_NODES, 0, step_axial, tables[0])[0]
    radius_node = radius_in + coordinates(RADIAL_NODES, 0, step_radial, tables[0])[0]
    radius_face = radius_in + jnp.arange(RADIAL_TOTAL + 1, dtype=jnp.int32).astype(jnp.float32) * step_radial
    inner_state = jnp.concatenate([density[None, :, :, :4], momentum[:, :, :, :4], energy[None, :, :, :4]], axis=0)
    wall_state = jnp.einsum('caxk,k->cax', inner_state, at_lower, precision=highest)
    wall_press = pressure_of(wall_state)
    flag_nodes = jnp.repeat(jnp.repeat(wall_flags.astype(jnp.float32), 4, axis=0), 4, axis=1)
    weight_azim = jnp.tile(weights, AZIM_TOTAL) * (0.5 * step_azim)
    weight_axial = jnp.tile(weights, AXIAL_TOTAL) * (0.5 * step_axial)
    node_area = radius_in * weight_azim[:, None] * weight_axial[None, :]
    pushed = flag_nodes * wall_press * node_area
    cos_col = jnp.cos(angle_node)[:, None]
    sin_col = jnp.sin(angle_node)[:, None]
    axial_row = axial_node[None, :]
    wall_loads = jnp.stack([-jnp.sum(pushed * cos_col), -jnp.sum(pushed * sin_col), jnp.sum(pushed * axial_row * sin_col), -jnp.sum(pushed * axial_row * cos_col)])
    body_next = rigid_update(body_motion, wall_loads)
    rates_next = body_next[3:]
    offsets = jnp.asarray((tables[0] + 1.0) / 2.0, jnp.float32)
    axial_col = axial_node[:, None, None, None]
    radius_col = radius_node[None, :, None, None]

    def slab_state(elem_index):
        begin_at = (elem_index * 4).astype(jnp.int32)
        return jnp.concatenate([lax.dynamic_slice_in_dim(density, begin_at, 4, 0)[None], lax.dynamic_slice_in_dim(momentum, begin_at, 4, 1), lax.dynamic_slice_in_dim(energy, begin_at, 4, 0)[None]], axis=0)

    def azim_line(slab):
        return jnp.moveaxis(slab, 1, -1)[:, :, :, None, :]

    def azim_normal(angle_pos):
        return (-jnp.sin(angle_pos), jnp.cos(angle_pos), 0.0)

    def slab_update(elem_index):
        prev_index = (elem_index + AZIM_TOTAL - 1) % AZIM_TOTAL
        next_index = (elem_index + 1) % AZIM_TOTAL
        current = slab_state(elem_index)
        elem_float = elem_index.astype(jnp.float32)
        angle_here = (elem_float + offsets) * step_azim
        angle_prev = (prev_index.astype(jnp.float32) + offsets) * step_azim
        angle_next = (next_index.astype(jnp.float32) + offsets) * step_azim
        angle_faces = jnp.stack([elem_float * step_azim, (elem_float + 1.0) * step_azim])
        prev_traces = line_traces(azim_line(slab_state(prev_index)), azim_normal(angle_prev), tables)
        next_traces = line_traces(azim_line(slab_state(next_index)), azim_normal(angle_next), tables)
        node_geo = (azim_normal(angle_here), azim_grid(body_next, angle_here, axial_col, radius_col), 1.0)
        face_geo = (azim_normal(angle_faces), azim_grid(body_next, angle_faces, axial_col[..., 0], radius_col[..., 0]), 1.0)
        dg_azim = line_residual(azim_line(current), node_geo, face_geo, (prev_traces[1], prev_traces[2]), (next_traces[0], next_traces[2]), tables)
        dg_azim = jnp.moveaxis(dg_azim[:, :, :, 0, :], -1, 1)
        angle_four = angle_here[:, None, None, None]
        radius_four = radius_node[None, :, None, None]
        axial_form = jnp.moveaxis(current, 2, -1).reshape(5, 4, RADIAL_NODES, AXIAL_TOTAL, 4)
        axial_speed = axial_grid(body_next, angle_four, radius_four)
        z_normal = (0.0, 0.0, 1.0)
        axial_ghost = (free_state((5, 4, RADIAL_NODES, 1)), free_speed(1.0))
        dg_axial = line_residual(axial_form, (z_normal, axial_speed, 1.0), (z_normal, axial_speed[..., 0], 1.0), axial_ghost, axial_ghost, tables)
        dg_axial = jnp.moveaxis(dg_axial.reshape(5, 4, RADIAL_NODES, AXIAL_NODES), -1, 2)
        axial_four = axial_node[None, :, None, None]
        radial_form = current.reshape(5, 4, AXIAL_NODES, RADIAL_TOTAL, 4)
        r_normal = (jnp.cos(angle_four), jnp.sin(angle_four), 0.0)
        radial_speed = radial_grid(body_next, angle_four, axial_four)
        node_geo_r = (r_normal, radial_speed, radius_node.reshape(RADIAL_TOTAL, 4))
        face_geo_r = ((r_normal[0][..., 0], r_normal[1][..., 0], 0.0), radial_speed[..., 0], radius_face)
        radial_ghost = (free_state((5, 4, AXIAL_NODES, 1)), free_speed(0.0))
        dg_radial = line_residual(radial_form, node_geo_r, face_geo_r, None, radial_ghost, tables)
        dg_radial = dg_radial.reshape(5, 4, AXIAL_NODES, RADIAL_NODES)
        residual = frame_source(current, rates_next) - (2.0 / step_radial * dg_radial + 2.0 / step_azim * dg_azim) / radius_node - 2.0 / step_axial * dg_axial
        increment = time_step * residual
        return (increment[0], increment[1:4], increment[4])
    out_dens, out_mom, out_ener = lax.map(slab_update, jnp.arange(AZIM_TOTAL, dtype=jnp.int32))
    density_change = out_dens.reshape(AZIM_NODES, AXIAL_NODES, RADIAL_NODES)
    momentum_change = jnp.moveaxis(out_mom, 1, 0).reshape(3, AZIM_NODES, AXIAL_NODES, RADIAL_NODES)
    energy_change = out_ener.reshape(AZIM_NODES, AXIAL_NODES, RADIAL_NODES)
    return (density_change, momentum_change, energy_change, body_next)
```

```python
import math

import jax
import jax.numpy as jnp
import numpy as np
from jax import lax
from jax.experimental import pallas as pl
from jax.experimental.pallas import tpu as pltpu
from jax.sharding import PartitionSpec as P

MESH = pl.DeviceIdType.MESH
F32 = jnp.float32

AZIM, AXIAL, RADIAL = 32, 8, 2
ROOT = 1
STEP_A = 2.0 * math.pi / 32
STEP_Z = 8.0 / 16
STEP_R = 2.0 / 64
DT = 0.05 * min(STEP_R, STEP_Z, STEP_A)
FREE = (1.0, 0.0, 0.0, 0.5, 1.0 / (1.4 * 0.4) + 0.125)


def fr_tables():
    outer_point = np.sqrt(3.0 / 7.0 + 2.0 / 7.0 * np.sqrt(6.0 / 5.0))
    inner_point = np.sqrt(3.0 / 7.0 - 2.0 / 7.0 * np.sqrt(6.0 / 5.0))
    points = np.array([-outer_point, -inner_point, inner_point, outer_point])
    outer_weight = (18.0 - np.sqrt(30.0)) / 36.0
    inner_weight = (18.0 + np.sqrt(30.0)) / 36.0
    weights = np.array([outer_weight, inner_weight, inner_weight, outer_weight])
    bary_weights = np.array(
        [1.0 / np.prod([points[i] - points[j] for j in range(4) if j != i]) for i in range(4)]
    )
    derivative = np.zeros((4, 4))
    for i in range(4):
        for j in range(4):
            if i != j:
                derivative[i, j] = bary_weights[j] / bary_weights[i] / (points[i] - points[j])
        derivative[i, i] = -np.sum(derivative[i])

    def basis_at(location):
        return np.array(
            [
                np.prod(
                    [(location - points[j]) / (points[i] - points[j]) for j in range(4) if j != i]
                )
                for i in range(4)
            ]
        )

    at_lower = basis_at(-1.0)
    at_upper = basis_at(1.0)
    third_slope = 0.5 * (15.0 * points * points - 3.0)
    fourth_slope = 0.5 * (35.0 * points**3 - 15.0 * points)
    slope_left = 0.5 * (fourth_slope - third_slope)
    slope_right = 0.5 * (fourth_slope + third_slope)
    return (points, weights, derivative, at_lower, at_upper, slope_left, slope_right)


X, Q, D, LA, LB, SC, SE = fr_tables()
OFF = (X + 1.0) / 2.0
MIX = D - np.outer(SC, LA) - np.outer(SE, LB)


def radial_matrices():
    low, up, mean_own, mean_below, mix, corr = (np.zeros((128, 128)) for _ in range(6))
    for j in range(128):
        e, k = divmod(j, 4)
        below = 31 if j == 127 else e - 1
        for i in range(4):
            low[4 * e + i, j] = LA[i]
            mean_own[4 * e + i, j] = Q[i] / 2
            mix[4 * e + i, j] = MIX[k, i]
            if below >= 0:
                up[4 * below + i, j] = LB[i]
                mean_below[4 * below + i, j] = Q[i] / 2
        corr[4 * e, j] += SC[k]
        corr[127 if e == 31 else 4 * (e + 1), j] += SE[k]
    return np.concatenate([low, up, mean_own, mean_below, mix, corr], axis=1).astype(np.float32)


def axial_matrices():
    low, up, mean_low, mean_up, mix, corr = (np.zeros((8, 8)) for _ in range(6))
    for j in range(8):
        e, k = divmod(j, 4)
        own = None if j == 3 else e
        below = 1 if j == 3 else (0 if e == 1 else None)
        for i in range(4):
            if own is not None:
                low[j, 4 * own + i] = LA[i]
                mean_low[j, 4 * own + i] = Q[i] / 2
            if below is not None:
                up[j, 4 * below + i] = LB[i]
                mean_up[j, 4 * below + i] = Q[i] / 2
            mix[j, 4 * e + i] = MIX[k, i]
        corr[j, 4 * e] += SC[k]
        corr[j, 4 if e == 0 else 3] += SE[k]
    pack, pack_mean = np.zeros((8, 32)), np.zeros((8, 32))
    for a in range(4):
        for i in range(4):
            pack[a, 8 * a + i] = LA[i]
            pack[4 + a, 8 * a + 4 + i] = LB[i]
            pack_mean[a, 8 * a + i] = Q[i] / 2
            pack_mean[4 + a, 8 * a + 4 + i] = Q[i] / 2
    four = np.eye(4)
    parts = [np.kron(four, low), np.kron(four, up), pack]
    parts += [np.kron(four, mean_low), np.kron(four, mean_up), pack_mean]
    parts += [np.kron(four, mix), np.kron(four, corr)]
    return np.concatenate(parts, axis=0).astype(np.float32)


def angle_table():
    table = np.zeros((32, 128))
    for e in range(32):
        angles = np.array([*(e + OFF), e, e + 1.0]) * STEP_A
        table[e, 0:6] = np.cos(angles)
        table[e, 6:12] = np.sin(angles)
    return table.astype(np.float32)


def dot(a, b):
    return jnp.dot(a, b, precision=lax.Precision.HIGHEST, preferred_element_type=F32)


def weighed(factors, values):
    total = float(factors[0]) * values[0]
    for factor, value in zip(factors[1:], values[1:]):
        total = total + float(factor) * value
    return total


def pressure_of(u):
    return 0.4 * (u[4] - 0.5 * (u[1] * u[1] + u[2] * u[2] + u[3] * u[3]) / u[0])


def still_flux(u, normal):
    p = pressure_of(u)
    through = u[3] if normal is None else u[1] * normal[0] + u[2] * normal[1]
    vn = through / u[0]
    flux = [through, u[1] * vn, u[2] * vn, u[3] * vn, (u[4] + p) * vn]
    if normal is None:
        flux[3] = flux[3] + p
    else:
        flux[1] = flux[1] + p * normal[0]
        flux[2] = flux[2] + p * normal[1]
    return flux


def face_terms(minus, plus, bound, normal):
    low, high = still_flux(minus, normal), still_flux(plus, normal)
    half_jump = [0.5 * (b - a) for a, b in zip(minus, plus)]
    mean = [0.5 * (a + b) for a, b in zip(minus, plus)]
    base = [0.5 * (a + b) - bound * h for a, b, h in zip(low, high, half_jump)]
    return base, mean, half_jump


def section_kernel(
    rho_h, mom_h, ene_h, flag_h, body_h, radm_h, axm_h, ang_h,
    out_ref, body_ref,
    u_v, radm, axm, ang_s, flag_s, body_s,
    own, col, p1, p2, p3,
    azs_lo, azs_hi, azr_lo, azr_hi, axs, axr_lo, axr_hi, rads, radr,
    r0, br, cr, bz, cz, aface,
    load_sem, send_sem, recv_sem, ready_sem,
):
    az, ax, ra = lax.axis_index("azim"), lax.axis_index("axial"), lax.axis_index("radial")
    is_root = (ra == 0) & (ax == ROOT)
    is_near = (ra == 0) & (ax < 4) & (ax != ROOT)
    is_far = (ra == 0) & (ax >= 4)
    column_root = {"axial": ROOT, "radial": 0}

    loads = [
        pltpu.make_async_copy(src, dst, load_sem.at[i])
        for i, (src, dst) in enumerate(
            [
                (ang_h.at[pl.ds(az, 1)], ang_s),
                (flag_h, flag_s),
                (rho_h, u_v.at[0]),
                (mom_h, u_v.at[pl.ds(1, 3)]),
                (ene_h, u_v.at[4]),
                (radm_h, radm),
                (axm_h, axm),
                (body_h, body_s),
            ]
        )
    ]
    for load in loads:
        load.start()

    barrier = pltpu.get_barrier_semaphore()

    def greet(device):
        pl.semaphore_signal(barrier, inc=1, device_id=device, device_id_type=MESH)

    @pl.when(is_root)
    def _():
        def greet_column(i, carry):
            for k in (7, 6, 5, 4):
                greet({"azim": i, "axial": k, "radial": 0})
            return carry

        lax.fori_loop(0, AZIM, greet_column, 0)

        def greet_root(i, carry):
            greet({"azim": lax.rem(az + i, AZIM)})
            return carry

        lax.fori_loop(1, AZIM, greet_root, 0)
        for k in (0, 2, 3):
            greet({"axial": k})
        for k in range(AXIAL):
            greet({"axial": k, "radial": 1})

    below = lax.rem(az + (AZIM - 1), AZIM)
    above = lax.rem(az + 1, AZIM)
    greet({"azim": below})
    greet({"azim": above})

    @pl.when(ax > 0)
    def _():
        greet({"axial": ax - 1})

    @pl.when(ax < AXIAL - 1)
    def _():
        greet({"axial": ax + 1})

    @pl.when(ra == 0)
    def _():
        greet({"radial": 1})

    sub = lax.broadcasted_iota(jnp.int32, (8, 128), 0)
    lane = lax.broadcasted_iota(jnp.int32, (8, 128), 1)
    lane32 = lax.broadcasted_iota(jnp.int32, (32, 128), 1)
    sub32 = lax.broadcasted_iota(jnp.int32, (32, 128), 0) & 7

    def by_place(place, values):
        out = jnp.full(place.shape, float(values[3]), F32)
        for k in range(3):
            out = jnp.where(place == k, float(values[k]), out)
        return out

    z = ((ax * 2 + (sub >> 2)).astype(F32) + by_place(sub & 3, OFF)) * STEP_Z
    elem_r = (ra * 32 + (lane >> 2)).astype(F32)
    r = 1.0 + (elem_r + by_place(lane & 3, OFF)) * STEP_R
    r_face = 1.0 + (elem_r + jnp.where(lane == 127, 1.0, 0.0)) * STEP_R

    loads[0].wait()
    loads[1].wait()
    cos = [ang_s[0, k] for k in range(6)]
    sin = [ang_s[0, 6 + k] for k in range(6)]
    flag = jnp.where(
        sub < 4,
        jnp.full((8, 128), flag_s[0, 0], jnp.int32),
        jnp.full((8, 128), flag_s[0, 1], jnp.int32),
    ).astype(F32)
    area_z = flag * by_place(sub & 3, Q * (0.5 * STEP_Z))
    zero = jnp.zeros((8, 128), F32)
    load_w = []
    for a in range(4):
        arm = jnp.where(lane >= 2, z, 1.0) * area_z * float(Q[a] * (0.5 * STEP_A))
        turn = jnp.where((lane == 0) | (lane == 3), -cos[a], jnp.where(lane == 1, -sin[a], sin[a]))
        load_w.append(jnp.where(lane < 4, arm * turn, zero))
    load_w = jnp.concatenate(load_w, axis=0)
    wall_a = jnp.where(lane32 < 4, by_place(lane32 & 3, LA), 0.0)
    loads[2].wait()
    loads[3].wait()
    loads[4].wait()
    u = [u_v[f].reshape(32, 128) for f in range(5)]

    wall = [jnp.sum(x * wall_a, axis=1, keepdims=True) for x in u]
    own[...] = jnp.sum(pressure_of(wall) * load_w, axis=0, keepdims=True)

    greeted = 2 + jnp.where(ax > 0, 1, 0) + jnp.where(ax < AXIAL - 1, 1, 0)
    greeted = greeted + jnp.where(
        ra == 1, 2, jnp.where(ax == ROOT, AZIM - 1, jnp.where(ax >= 4, AZIM, 1))
    )
    pl.semaphore_wait(barrier, greeted)

    def push(src, dst, lane_of, device):
        return pltpu.make_async_remote_copy(
            src_ref=src,
            dst_ref=dst,
            send_sem=send_sem.at[lane_of],
            recv_sem=recv_sem.at[lane_of],
            device_id=device,
            device_id_type=MESH,
        )

    def arrived(ref, lane_of):
        pltpu.make_async_copy(ref, ref, recv_sem.at[lane_of]).wait()

    def left(ref, lane_of):
        pltpu.make_async_copy(ref, ref, send_sem.at[lane_of]).wait()

    @pl.when(is_far)
    def _():
        slot = az * 4 + (ax - 4)

        def send(i, carry):
            push(own, p2.at[slot], 1, {"azim": i, "axial": ROOT, "radial": 0}).start()
            return carry

        lax.fori_loop(0, AZIM, send, 0)

    @pl.when(is_near)
    def _():
        push(own, p1.at[jnp.where(ax == 0, 0, ax - 1)], 0, column_root).start()

    @pl.when(jnp.logical_not(is_root))
    def _():
        pl.semaphore_signal(ready_sem, inc=1, device_id=column_root, device_id_type=MESH)

    rho = u[0]
    p = pressure_of(u)
    sound = jnp.sqrt(1.4 * p / rho)
    cos32 = jnp.concatenate([jnp.full((8, 128), cos[a], F32) for a in range(4)], axis=0)
    sin32 = jnp.concatenate([jnp.full((8, 128), sin[a], F32) for a in range(4)], axis=0)
    speed_r = jnp.abs((u[1] * cos32 + u[2] * sin32) / rho) + sound
    speed_a = jnp.abs((u[2] * cos32 - u[1] * sin32) / rho) + sound
    speed_z = jnp.abs(u[3] / rho) + sound

    def rows(x):
        return [x[8 * a : 8 * a + 8] for a in range(4)]

    u_rows = [rows(x) for x in u]
    mean_a = weighed(Q / 2, rows(speed_a))
    for f in range(5):
        azs_lo[f] = weighed(LA, u_rows[f])
        azs_hi[f] = weighed(LB, u_rows[f])
    azs_lo[5] = mean_a
    azs_hi[5] = mean_a
    push(azs_lo, azr_hi, 3, {"azim": below}).start()
    push(azs_hi, azr_lo, 4, {"azim": above}).start()

    loads[5].wait()
    loads[6].wait()
    u_wide = jnp.concatenate(u, axis=1)
    ax_tr = dot(axm[0:72], u_wide)
    ax_sp = dot(axm[72:144], speed_z)
    for f in range(5):
        axs[f] = ax_tr[64:72, 128 * f : 128 * (f + 1)]
    axs[5] = ax_sp[64:72]

    @pl.when(ax > 0)
    def _():
        push(axs, axr_hi, 5, {"axial": ax - 1}).start()

    @pl.when(ax < AXIAL - 1)
    def _():
        push(axs, axr_lo, 6, {"axial": ax + 1}).start()

    rad_tr = dot(jnp.concatenate(u, axis=0), radm[:, 0:256])
    rad_sp = dot(speed_r, radm[:, 256:512])
    rad_lo = [rad_tr[32 * f : 32 * f + 32, 0:128] for f in range(5)] + [rad_sp[:, 0:128]]
    rad_up = [rad_tr[32 * f : 32 * f + 32, 128:256] for f in range(5)] + [rad_sp[:, 128:256]]
    inner = jnp.full((32, 128), ra, jnp.int32) == 0
    packed = jnp.zeros((32, 128), F32)
    for f in range(6):
        edge = jnp.where(
            inner,
            jnp.broadcast_to(rad_up[f][:, 127:128], (32, 128)),
            jnp.broadcast_to(rad_lo[f][:, 0:1], (32, 128)),
        )
        packed = jnp.where(lane32 == f, edge, packed)
    rads[...] = packed

    @pl.when(ra == 1)
    def _():
        push(rads, radr, 7, {"radial": 0}).start()

    r32 = jnp.concatenate([r] * 4, axis=0)
    rf32 = jnp.concatenate([r_face] * 4, axis=0)
    k_r = (DT * 2.0 / STEP_R) / r32
    k_a = (DT * 2.0 / STEP_A) / r
    k_a32 = jnp.concatenate([k_a] * 4, axis=0)
    k_z = DT * 2.0 / STEP_Z
    flux_r = still_flux(u, (cos32, sin32))
    flux_a = still_flux(u, (-sin32, cos32))
    flux_z = still_flux(u, None)
    mix_r = dot(
        jnp.concatenate([r32 * x for x in flux_r] + [r32 * x for x in u], axis=0), radm[:, 512:640]
    )
    mix_z = dot(axm[144:176], jnp.concatenate(flux_z + u, axis=1))
    for f in range(5):
        flux_rows = rows(flux_a[f])
        mix_a = jnp.concatenate([weighed(MIX[a], flux_rows) for a in range(4)], axis=0)
        r0[f] = (
            -k_r * mix_r[32 * f : 32 * f + 32]
            - k_a32 * mix_a
            - k_z * mix_z[:, 128 * f : 128 * f + 128]
        )
        br[f] = k_r * mix_r[160 + 32 * f : 192 + 32 * f]
        bz[f] = k_z * mix_z[:, 640 + 128 * f : 768 + 128 * f]

    @pl.when(is_root)
    def _():
        arrived(p1, 0)
        col[...] = own[...] + jnp.sum(p1[...], axis=0)

        def send(i, carry):
            push(col, p2.at[4 * AZIM - 1 + i], 1, {"azim": lax.rem(az + i, AZIM)}).start()
            return carry

        lax.fori_loop(1, AZIM, send, 0)

    arrived(azr_lo, 4)
    arrived(azr_hi, 3)
    own_lo = [azs_lo[f] for f in range(6)]
    own_hi = [azs_hi[f] for f in range(6)]
    from_lo = [azr_lo[f] for f in range(6)]
    from_hi = [azr_hi[f] for f in range(6)]
    lo_terms = face_terms(
        from_lo[:5], own_lo[:5], jnp.maximum(from_lo[5], own_lo[5]), (-sin[4], cos[4])
    )
    hi_terms = face_terms(
        own_hi[:5], from_hi[:5], jnp.maximum(from_hi[5], own_hi[5]), (-sin[5], cos[5])
    )
    for f in range(5):
        for a in range(4):
            fix = float(SC[a]) * lo_terms[0][f] + float(SE[a]) * hi_terms[0][f]
            r0[f, 8 * a : 8 * a + 8] = r0[f, 8 * a : 8 * a + 8] - k_a * fix
        aface[f] = k_a * lo_terms[1][f]
        aface[5 + f] = k_a * lo_terms[2][f]
        aface[10 + f] = k_a * hi_terms[1][f]
        aface[15 + f] = k_a * hi_terms[2][f]

    @pl.when(ax > 0)
    def _():
        arrived(axr_lo, 6)

    @pl.when(ax == 0)
    def _():
        for f in range(6):
            axr_lo[f] = jnp.full((8, 128), (*FREE, 1.5)[f], F32)

    @pl.when(ax < AXIAL - 1)
    def _():
        arrived(axr_hi, 5)

    @pl.when(ax == AXIAL - 1)
    def _():
        for f in range(6):
            axr_hi[f] = jnp.full((8, 128), (*FREE, 1.5)[f], F32)

    def spread(ref, f, first):
        got = ref[f]
        return jnp.concatenate(
            [jnp.broadcast_to(got[first + a : first + a + 1], (8, 128)) for a in range(4)], axis=0
        )

    minus, plus = [], []
    for f in range(6):
        if f < 5:
            low, up = (ax_tr[32 * i : 32 * i + 32, 128 * f : 128 * f + 128] for i in range(2))
        else:
            low, up = ax_sp[0:32], ax_sp[32:64]
        minus.append(jnp.where(sub32 < 3, spread(axr_lo, f, 4), up))
        plus.append(jnp.where(sub32 == 3, spread(axr_hi, f, 0), low))
    terms = face_terms(minus[:5], plus[:5], jnp.maximum(minus[5], plus[5]), None)
    fix_z = dot(axm[176:208], jnp.concatenate(terms[0] + terms[1] + terms[2], axis=1))
    for f in range(5):
        r0[f] = r0[f] - k_z * fix_z[:, 128 * f : 128 * f + 128]
        bz[f] = bz[f] + k_z * fix_z[:, 640 + 128 * f : 768 + 128 * f]
        cz[f] = k_z * fix_z[:, 1280 + 128 * f : 1408 + 128 * f]

    arrived(radr, 7)

    @pl.when(ra == 0)
    def _():
        push(rads, radr, 7, {"radial": 1}).start()

    lowest = lane32 < 4
    highest = lane32 == 127
    minus, plus = [], []
    got = radr[...]
    for f in range(6):
        ghost = jnp.broadcast_to(got[:, f : f + 1], (32, 128))
        minus.append(jnp.where(lowest, jnp.where(inner, rad_lo[f], ghost), rad_up[f]))
        free = (*FREE, 1.0)[f]
        plus.append(jnp.where(highest, jnp.where(inner, ghost, free), rad_lo[f]))
    base, mean, half_jump = face_terms(
        minus[:5], plus[:5], jnp.maximum(minus[5], plus[5]), (cos32, sin32)
    )
    at_wall = lowest & inner
    pw = pressure_of(plus[:5])
    wall_base = [0.0, pw * cos32, pw * sin32, 0.0, 0.0]
    wall_mean = [0.0, 0.0, 0.0, 0.0, -pw]
    base = [rf32 * jnp.where(at_wall, w, x) for w, x in zip(wall_base, base)]
    mean = [rf32 * jnp.where(at_wall, w, x) for w, x in zip(wall_mean, mean)]
    half_jump = [rf32 * jnp.where(at_wall, 0.0, x) for x in half_jump]
    fix_r = dot(jnp.concatenate(base + mean + half_jump, axis=0), radm[:, 640:768])
    for f in range(5):
        r0[f] = r0[f] - k_r * fix_r[32 * f : 32 * f + 32]
        br[f] = br[f] + k_r * fix_r[160 + 32 * f : 192 + 32 * f]
        cr[f] = k_r * fix_r[320 + 32 * f : 352 + 32 * f]

    loads[7].wait()

    @pl.when(is_root)
    def _():
        pl.semaphore_wait(ready_sem, 2 * AXIAL - 1)
        arrived(p2, 1)
        p3[...] = col[...] + jnp.sum(p2[...], axis=0)
        for k in (2, 0, 3, 4, 5, 6, 7):
            push(p3, p3, 2, {"axial": k}).start()
        for k in range(AXIAL):
            push(p3, p3, 2, {"axial": k, "radial": 1}).start()

    @pl.when(jnp.logical_not(is_root))
    def _():
        arrived(p3, 2)

    total = p3[...]
    load = [jnp.broadcast_to(total[:, i : i + 1], (8, 128)) for i in range(4)]
    v = [body_s[0, i] for i in range(3)]
    om = [body_s[0, 3 + i] for i in range(3)]
    spin = [om[0], om[1], 0.25 * om[2]]
    gyro = [
        om[1] * spin[2] - om[2] * spin[1],
        om[2] * spin[0] - om[0] * spin[2],
        om[0] * spin[1] - om[1] * spin[0],
    ]
    v0 = v[0] + 60.0 * load[0]
    v1 = v[1] + 60.0 * load[1]
    v2 = jnp.full((8, 128), v[2], F32)
    o0 = om[0] + 30.0 * (load[2] - gyro[0])
    o1 = om[1] + 30.0 * (load[3] - gyro[1])
    o2 = jnp.full((8, 128), om[2] - 120.0 * gyro[2], F32)
    body_row = zero
    for i, value in enumerate((v0, v1, v2, o0, o1, o2)):
        body_row = jnp.where(lane == i, value, body_row)
    body_ref[...] = body_row[0:1, 0:6]

    along_x = v0 + z * o1
    along_y = v1 - z * o0
    swirl = o2 * r

    def azim_speed(k):
        return cos[k] * along_y - sin[k] * along_x + swirl

    s_a = [azim_speed(k) for k in range(4)]
    s_lo, s_hi = azim_speed(4), azim_speed(5)
    s_r = [cos[a] * along_x + sin[a] * along_y for a in range(4)]
    s_z = [v2 + r * (o0 * sin[a] - o1 * cos[a]) for a in range(4)]
    d0, d1, d2 = DT * o0, DT * o1, DT * o2
    for f in range(5):
        carried = [k_a * s_a[k] * u_v[f, k] for k in range(4)]
        at_lo = s_lo * aface[f] + jnp.abs(s_lo) * aface[5 + f]
        at_hi = s_hi * aface[10 + f] + jnp.abs(s_hi) * aface[15 + f]
        for a in range(4):
            row = slice(8 * a, 8 * a + 8)
            value = r0[f, row] + s_r[a] * br[f, row] + jnp.abs(s_r[a]) * cr[f, row]
            value = value + s_z[a] * bz[f, row] + jnp.abs(s_z[a]) * cz[f, row]
            value = value + weighed(MIX[a], carried)
            value = value + float(SC[a]) * at_lo + float(SE[a]) * at_hi
            if f == 1:
                value = value - (d1 * u_v[3, a] - d2 * u_v[2, a])
            if f == 2:
                value = value - (d2 * u_v[1, a] - d0 * u_v[3, a])
            if f == 3:
                value = value - (d0 * u_v[2, a] - d1 * u_v[1, a])
            out_ref[f, a] = value

    @pl.when(is_root)
    def _():
        left(p2.at[pl.ds(0, AZIM - 1)], 1)
        left(p2.at[pl.ds(0, 2 * AXIAL - 1)], 2)

    @pl.when(is_far)
    def _():
        left(p2.at[pl.ds(0, AZIM)], 1)

    @pl.when(is_near)
    def _():
        left(own, 0)

    left(azs_lo, 3)
    left(azs_hi, 4)

    @pl.when(ax > 0)
    def _():
        left(axs, 5)

    @pl.when(ax < AXIAL - 1)
    def _():
        left(axs, 6)

    left(rads, 7)


def store_kernel(out_ref, body_ref, rho_h, mom_h, ene_h, body_h, sems):
    copies = [
        pltpu.make_async_copy(src, dst, sems.at[i])
        for i, (src, dst) in enumerate(
            [
                (out_ref.at[pl.ds(1, 3)], mom_h),
                (out_ref.at[0], rho_h),
                (out_ref.at[4], ene_h),
                (body_ref, body_h),
            ]
        )
    ]
    for copy in copies:
        copy.start()
    for copy in copies:
        copy.wait()


def on_device(density, momentum, energy, wall_flags, body_motion):
    block = density.shape
    hbm = pl.BlockSpec(memory_space=pl.ANY)
    vmem = pl.BlockSpec(memory_space=pltpu.VMEM)
    halo = pltpu.VMEM((6, 8, 128), F32)
    part = pltpu.VMEM((5, 32, 128), F32)
    increment, body_row = pl.pallas_call(
        section_kernel,
        out_shape=(pltpu.VMEM((5, *block), F32), pltpu.VMEM((1, 6), F32)),
        in_specs=[hbm] * 8,
        out_specs=(vmem, vmem),
        scratch_shapes=[
            pltpu.VMEM((5, *block), F32),
            pltpu.VMEM((128, 768), F32),
            pltpu.VMEM((208, 32), F32),
            pltpu.SMEM((1, 128), F32),
            pltpu.SMEM((1, 2), jnp.int32),
            pltpu.SMEM((1, 6), F32),
            pltpu.VMEM((1, 128), F32),
            pltpu.VMEM((1, 128), F32),
            pltpu.VMEM((3, 1, 128), F32),
            pltpu.VMEM((5 * AZIM - 1, 1, 128), F32),
            pltpu.VMEM((1, 128), F32),
            *[halo] * 7,
            pltpu.VMEM((32, 128), F32),
            pltpu.VMEM((32, 128), F32),
            *[part] * 5,
            pltpu.VMEM((20, 8, 128), F32),
            pltpu.SemaphoreType.DMA((8,)),
            pltpu.SemaphoreType.DMA((8,)),
            pltpu.SemaphoreType.DMA((8,)),
            pltpu.SemaphoreType.REGULAR,
        ],
        compiler_params=pltpu.CompilerParams(
            collective_id=0, has_side_effects=True
        ),
    )(
        density,
        momentum,
        energy,
        wall_flags,
        body_motion.reshape(1, 6),
        jnp.asarray(radial_matrices()),
        jnp.asarray(axial_matrices()),
        jnp.asarray(angle_table()),
    )
    increment = pltpu.with_memory_space_constraint(increment, pltpu.VMEM)
    body_row = pltpu.with_memory_space_constraint(body_row, pltpu.VMEM)
    rho, mom, ene, body = pl.pallas_call(
        store_kernel,
        out_shape=(
            jax.ShapeDtypeStruct(block, F32),
            jax.ShapeDtypeStruct((3, *block), F32),
            jax.ShapeDtypeStruct(block, F32),
            jax.ShapeDtypeStruct((1, 6), F32),
        ),
        in_specs=[vmem, vmem],
        out_specs=[hbm] * 4,
        scratch_shapes=[pltpu.SemaphoreType.DMA((4,))],
    )(increment, body_row)
    return rho, mom, ene, body.reshape(6)


def solution(mesh):
    return jax.shard_map(
        on_device,
        mesh=mesh,
        in_specs=(
            P("azim", "axial", "radial"),
            P(None, "azim", "axial", "radial"),
            P("azim", "axial", "radial"),
            P("azim", "axial"),
            P(),
        ),
        out_specs=(
            P("azim", "axial", "radial"),
            P(None, "azim", "axial", "radial"),
            P("azim", "axial", "radial"),
            P(),
        ),
        check_vma=False,
    )
```

```python
import math

import jax
import jax.numpy as jnp
import numpy as np
from jax import lax
from jax.experimental import pallas as pl
from jax.experimental.pallas import tpu as pltpu
from jax.sharding import PartitionSpec as P

MESH = pl.DeviceIdType.MESH
F32 = jnp.float32

AZIM, AXIAL, RADIAL = 32, 8, 2
ROOT = 1
STEP_A = 2.0 * math.pi / 32
STEP_Z = 8.0 / 16
STEP_R = 2.0 / 64
DT = 0.05 * min(STEP_R, STEP_Z, STEP_A)
FREE = (1.0, 0.0, 0.0, 0.5, 1.0 / (1.4 * 0.4) + 0.125)


def fr_tables():
    outer_point = np.sqrt(3.0 / 7.0 + 2.0 / 7.0 * np.sqrt(6.0 / 5.0))
    inner_point = np.sqrt(3.0 / 7.0 - 2.0 / 7.0 * np.sqrt(6.0 / 5.0))
    points = np.array([-outer_point, -inner_point, inner_point, outer_point])
    outer_weight = (18.0 - np.sqrt(30.0)) / 36.0
    inner_weight = (18.0 + np.sqrt(30.0)) / 36.0
    weights = np.array([outer_weight, inner_weight, inner_weight, outer_weight])
    bary_weights = np.array(
        [1.0 / np.prod([points[i] - points[j] for j in range(4) if j != i]) for i in range(4)]
    )
    derivative = np.zeros((4, 4))
    for i in range(4):
        for j in range(4):
            if i != j:
                derivative[i, j] = bary_weights[j] / bary_weights[i] / (points[i] - points[j])
        derivative[i, i] = -np.sum(derivative[i])

    def basis_at(location):
        return np.array(
            [
                np.prod(
                    [(location - points[j]) / (points[i] - points[j]) for j in range(4) if j != i]
                )
                for i in range(4)
            ]
        )

    at_lower = basis_at(-1.0)
    at_upper = basis_at(1.0)
    third_slope = 0.5 * (15.0 * points * points - 3.0)
    fourth_slope = 0.5 * (35.0 * points**3 - 15.0 * points)
    slope_left = 0.5 * (fourth_slope - third_slope)
    slope_right = 0.5 * (fourth_slope + third_slope)
    return (points, weights, derivative, at_lower, at_upper, slope_left, slope_right)


X, Q, D, LA, LB, SC, SE = fr_tables()
OFF = (X + 1.0) / 2.0
MIX = D - np.outer(SC, LA) - np.outer(SE, LB)


def radial_matrices():
    low, up, mean_own, mean_below, mix, corr = (np.zeros((128, 128)) for _ in range(6))
    for j in range(128):
        e, k = divmod(j, 4)
        below = 31 if j == 127 else e - 1
        for i in range(4):
            low[4 * e + i, j] = LA[i]
            mean_own[4 * e + i, j] = Q[i] / 2
            mix[4 * e + i, j] = MIX[k, i]
            if below >= 0:
                up[4 * below + i, j] = LB[i]
                mean_below[4 * below + i, j] = Q[i] / 2
        corr[4 * e, j] += SC[k]
        corr[127 if e == 31 else 4 * (e + 1), j] += SE[k]
    return np.concatenate([low, up, mean_own, mean_below, mix, corr], axis=1).astype(np.float32)


def axial_matrices():
    low, up, mean_low, mean_up, mix, corr = (np.zeros((8, 8)) for _ in range(6))
    for j in range(8):
        e, k = divmod(j, 4)
        own = None if j == 3 else e
        below = 1 if j == 3 else (0 if e == 1 else None)
        for i in range(4):
            if own is not None:
                low[j, 4 * own + i] = LA[i]
                mean_low[j, 4 * own + i] = Q[i] / 2
            if below is not None:
                up[j, 4 * below + i] = LB[i]
                mean_up[j, 4 * below + i] = Q[i] / 2
            mix[j, 4 * e + i] = MIX[k, i]
        corr[j, 4 * e] += SC[k]
        corr[j, 4 if e == 0 else 3] += SE[k]
    pack, pack_mean = np.zeros((8, 32)), np.zeros((8, 32))
    for a in range(4):
        for i in range(4):
            pack[a, 8 * a + i] = LA[i]
            pack[4 + a, 8 * a + 4 + i] = LB[i]
            pack_mean[a, 8 * a + i] = Q[i] / 2
            pack_mean[4 + a, 8 * a + 4 + i] = Q[i] / 2
    four = np.eye(4)
    parts = [np.kron(four, low), np.kron(four, up), pack]
    parts += [np.kron(four, mean_low), np.kron(four, mean_up), pack_mean]
    parts += [np.kron(four, mix), np.kron(four, corr)]
    return np.concatenate(parts, axis=0).astype(np.float32)


def angle_table():
    table = np.zeros((32, 128))
    for e in range(32):
        angles = np.array([*(e + OFF), e, e + 1.0]) * STEP_A
        table[e, 0:6] = np.cos(angles)
        table[e, 6:12] = np.sin(angles)
    return table.astype(np.float32)


def dot(a, b):
    return jnp.dot(a, b, precision=lax.Precision.HIGHEST, preferred_element_type=F32)


def weighed(factors, values):
    total = float(factors[0]) * values[0]
    for factor, value in zip(factors[1:], values[1:]):
        total = total + float(factor) * value
    return total


def pressure_of(u):
    return 0.4 * (u[4] - 0.5 * (u[1] * u[1] + u[2] * u[2] + u[3] * u[3]) / u[0])


def still_flux(u, normal):
    p = pressure_of(u)
    through = u[3] if normal is None else u[1] * normal[0] + u[2] * normal[1]
    vn = through / u[0]
    flux = [through, u[1] * vn, u[2] * vn, u[3] * vn, (u[4] + p) * vn]
    if normal is None:
        flux[3] = flux[3] + p
    else:
        flux[1] = flux[1] + p * normal[0]
        flux[2] = flux[2] + p * normal[1]
    return flux


def face_terms(minus, plus, bound, normal):
    low, high = still_flux(minus, normal), still_flux(plus, normal)
    half_jump = [0.5 * (b - a) for a, b in zip(minus, plus)]
    mean = [0.5 * (a + b) for a, b in zip(minus, plus)]
    base = [0.5 * (a + b) - bound * h for a, b, h in zip(low, high, half_jump)]
    return base, mean, half_jump


def section_kernel(
    rho_h, mom_h, ene_h, flag_h, body_h, radm_h, axm_h, ang_h,
    out_ref, body_ref,
    u_v, radm, axm, ang_s, flag_s, body_s,
    own, col, p1, p2, p3,
    azs_lo, azs_hi, azr_lo, azr_hi, axs, axr_lo, axr_hi, rads, radr,
    r0, br, cr, bz, cz, aface,
    load_sem, send_sem, recv_sem, ready_sem,
):
    az, ax, ra = lax.axis_index("azim"), lax.axis_index("axial"), lax.axis_index("radial")
    is_root = (ra == 0) & (ax == ROOT)
    is_relay = (ra == 0) & (ax == 0)
    is_near = (ra == 0) & (ax < 4) & (ax != ROOT)
    is_far = (ra == 0) & (ax >= 4)
    is_even = lax.rem(az, 2) == 0
    on_odd_core = lax.rem(ax, 2) == 1
    column_root = {"axial": ROOT, "radial": 0}

    loads = [
        pltpu.make_async_copy(src, dst, load_sem.at[i])
        for i, (src, dst) in enumerate(
            [
                (ang_h.at[pl.ds(az, 1)], ang_s),
                (flag_h, flag_s),
                (rho_h, u_v.at[0]),
                (mom_h, u_v.at[pl.ds(1, 3)]),
                (ene_h, u_v.at[4]),
                (radm_h, radm),
                (axm_h, axm),
                (body_h, body_s),
            ]
        )
    ]
    for load in loads:
        load.start()

    barrier = pltpu.get_barrier_semaphore()

    def greet(device):
        pl.semaphore_signal(barrier, inc=1, device_id=device, device_id_type=MESH)

    @pl.when(is_root)
    def _():
        def greet_column(i, carry):
            for k in (7, 6, 5, 4):
                greet({"azim": i, "axial": k, "radial": 0})
            return carry

        lax.fori_loop(0, AZIM, greet_column, 0)

        def greet_root(i, carry):
            greet({"azim": lax.rem(az + i, AZIM)})
            return carry

        lax.fori_loop(1, AZIM, greet_root, 0)
        for k in (0, 2, 3):
            greet({"axial": k})
        for k in range(AXIAL):
            greet({"axial": k, "radial": 1})

    below = lax.rem(az + (AZIM - 1), AZIM)
    above = lax.rem(az + 1, AZIM)
    @pl.when(is_even)
    def _():
        greet({"azim": below})
        greet({"azim": above})

    @pl.when(on_odd_core)
    def _():
        greet({"axial": ax - 1})

    @pl.when(on_odd_core & (ax < AXIAL - 1))
    def _():
        greet({"axial": ax + 1})

    @pl.when(ra == 0)
    def _():
        greet({"radial": 1})

    sub = lax.broadcasted_iota(jnp.int32, (8, 128), 0)
    lane = lax.broadcasted_iota(jnp.int32, (8, 128), 1)
    lane32 = lax.broadcasted_iota(jnp.int32, (32, 128), 1)
    sub32 = lax.broadcasted_iota(jnp.int32, (32, 128), 0) & 7

    def by_place(place, values):
        out = jnp.full(place.shape, float(values[3]), F32)
        for k in range(3):
            out = jnp.where(place == k, float(values[k]), out)
        return out

    z = ((ax * 2 + (sub >> 2)).astype(F32) + by_place(sub & 3, OFF)) * STEP_Z
    elem_r = (ra * 32 + (lane >> 2)).astype(F32)
    r = 1.0 + (elem_r + by_place(lane & 3, OFF)) * STEP_R
    r_face = 1.0 + (elem_r + jnp.where(lane == 127, 1.0, 0.0)) * STEP_R

    loads[0].wait()
    loads[1].wait()
    cos = [ang_s[0, k] for k in range(6)]
    sin = [ang_s[0, 6 + k] for k in range(6)]
    flag = jnp.where(
        sub < 4,
        jnp.full((8, 128), flag_s[0, 0], jnp.int32),
        jnp.full((8, 128), flag_s[0, 1], jnp.int32),
    ).astype(F32)
    area_z = flag * by_place(sub & 3, Q * (0.5 * STEP_Z))
    zero = jnp.zeros((8, 128), F32)
    load_w = []
    for a in range(4):
        arm = jnp.where(lane >= 2, z, 1.0) * area_z * float(Q[a] * (0.5 * STEP_A))
        turn = jnp.where((lane == 0) | (lane == 3), -cos[a], jnp.where(lane == 1, -sin[a], sin[a]))
        load_w.append(jnp.where(lane < 4, arm * turn, zero))
    load_w = jnp.concatenate(load_w, axis=0)
    wall_a = jnp.where(lane32 < 4, by_place(lane32 & 3, LA), 0.0)
    loads[2].wait()
    loads[3].wait()
    loads[4].wait()
    u = [u_v[f].reshape(32, 128) for f in range(5)]

    wall = [jnp.sum(x * wall_a, axis=1, keepdims=True) for x in u]
    own[...] = jnp.sum(pressure_of(wall) * load_w, axis=0, keepdims=True)

    greeted = jnp.where(is_even, 0, 2)
    greeted = greeted + jnp.where(on_odd_core, 0, jnp.where(ax > 0, 2, 1))
    greeted = greeted + jnp.where(
        ra == 1, 2, jnp.where(ax == ROOT, AZIM - 1, jnp.where(ax >= 4, AZIM, 1))
    )
    pl.semaphore_wait(barrier, greeted)

    def push(src, dst, lane_of, device):
        return pltpu.make_async_remote_copy(
            src_ref=src,
            dst_ref=dst,
            send_sem=send_sem.at[lane_of],
            recv_sem=recv_sem.at[lane_of],
            device_id=device,
            device_id_type=MESH,
        )

    def arrived(ref, lane_of):
        pltpu.make_async_copy(ref, ref, recv_sem.at[lane_of]).wait()

    def left(ref, lane_of):
        pltpu.make_async_copy(ref, ref, send_sem.at[lane_of]).wait()

    @pl.when(is_far)
    def _():
        slot = az * 4 + (ax - 4)

        def send(i, carry):
            push(own, p2.at[slot], 1, {"azim": i, "axial": ROOT, "radial": 0}).start()
            return carry

        lax.fori_loop(0, AZIM, send, 0)

    @pl.when(is_near)
    def _():
        push(own, p1.at[jnp.where(ax == 0, 0, ax - 1)], 0, column_root).start()

    @pl.when(jnp.logical_not(is_root))
    def _():
        pl.semaphore_signal(ready_sem, inc=1, device_id=column_root, device_id_type=MESH)

    rho = u[0]
    p = pressure_of(u)
    sound = jnp.sqrt(1.4 * p / rho)
    cos32 = jnp.concatenate([jnp.full((8, 128), cos[a], F32) for a in range(4)], axis=0)
    sin32 = jnp.concatenate([jnp.full((8, 128), sin[a], F32) for a in range(4)], axis=0)
    speed_r = jnp.abs((u[1] * cos32 + u[2] * sin32) / rho) + sound
    speed_a = jnp.abs((u[2] * cos32 - u[1] * sin32) / rho) + sound
    speed_z = jnp.abs(u[3] / rho) + sound

    def rows(x):
        return [x[8 * a : 8 * a + 8] for a in range(4)]

    u_rows = [rows(x) for x in u]
    mean_a = weighed(Q / 2, rows(speed_a))
    for f in range(5):
        azs_lo[f] = weighed(LA, u_rows[f])
        azs_hi[f] = weighed(LB, u_rows[f])
    azs_lo[5] = mean_a
    azs_hi[5] = mean_a

    def push_azim():
        push(azs_lo, azr_hi, 3, {"azim": below}).start()
        push(azs_hi, azr_lo, 4, {"azim": above}).start()

    pl.when(jnp.logical_not(is_even))(push_azim)

    loads[5].wait()
    loads[6].wait()
    u_wide = jnp.concatenate(u, axis=1)
    ax_tr = dot(axm[0:72], u_wide)
    ax_sp = dot(axm[72:144], speed_z)
    for f in range(5):
        axs[f] = ax_tr[64:72, 128 * f : 128 * (f + 1)]
    axs[5] = ax_sp[64:72]

    def push_axial_down():
        push(axs, axr_hi, 5, {"axial": ax - 1}).start()

    def push_axial_up():
        push(axs, axr_lo, 6, {"axial": ax + 1}).start()

    pl.when(jnp.logical_not(on_odd_core) & (ax > 0))(push_axial_down)
    pl.when(jnp.logical_not(on_odd_core))(push_axial_up)

    rad_tr = dot(jnp.concatenate(u, axis=0), radm[:, 0:256])
    rad_sp = dot(speed_r, radm[:, 256:512])
    rad_lo = [rad_tr[32 * f : 32 * f + 32, 0:128] for f in range(5)] + [rad_sp[:, 0:128]]
    rad_up = [rad_tr[32 * f : 32 * f + 32, 128:256] for f in range(5)] + [rad_sp[:, 128:256]]
    inner = jnp.full((32, 128), ra, jnp.int32) == 0
    packed = jnp.zeros((32, 128), F32)
    for f in range(6):
        edge = jnp.where(
            inner,
            jnp.broadcast_to(rad_up[f][:, 127:128], (32, 128)),
            jnp.broadcast_to(rad_lo[f][:, 0:1], (32, 128)),
        )
        packed = jnp.where(lane32 == f, edge, packed)
    rads[...] = packed

    @pl.when(ra == 1)
    def _():
        push(rads, radr, 7, {"radial": 0}).start()

    @pl.when(is_root)
    def _():
        arrived(p1, 0)
        col[...] = own[...] + jnp.sum(p1[...], axis=0)

        def send(i, carry):
            push(col, p2.at[4 * AZIM - 1 + i], 1, {"azim": lax.rem(az + i, AZIM)}).start()
            return carry

        lax.fori_loop(1, AZIM, send, 0)

    r32 = jnp.concatenate([r] * 4, axis=0)
    rf32 = jnp.concatenate([r_face] * 4, axis=0)
    k_r = (DT * 2.0 / STEP_R) / r32
    k_a = (DT * 2.0 / STEP_A) / r
    k_a32 = jnp.concatenate([k_a] * 4, axis=0)
    k_z = DT * 2.0 / STEP_Z
    flux_r = still_flux(u, (cos32, sin32))
    flux_a = still_flux(u, (-sin32, cos32))
    flux_z = still_flux(u, None)
    mix_r = dot(
        jnp.concatenate([r32 * x for x in flux_r] + [r32 * x for x in u], axis=0), radm[:, 512:640]
    )
    mix_z = dot(axm[144:176], jnp.concatenate(flux_z + u, axis=1))
    for f in range(5):
        flux_rows = rows(flux_a[f])
        mix_a = jnp.concatenate([weighed(MIX[a], flux_rows) for a in range(4)], axis=0)
        r0[f] = (
            -k_r * mix_r[32 * f : 32 * f + 32]
            - k_a32 * mix_a
            - k_z * mix_z[:, 128 * f : 128 * f + 128]
        )
        br[f] = k_r * mix_r[160 + 32 * f : 192 + 32 * f]
        bz[f] = k_z * mix_z[:, 640 + 128 * f : 768 + 128 * f]

    arrived(azr_lo, 4)
    arrived(azr_hi, 3)
    pl.when(is_even)(push_azim)
    own_lo = [azs_lo[f] for f in range(6)]
    own_hi = [azs_hi[f] for f in range(6)]
    from_lo = [azr_lo[f] for f in range(6)]
    from_hi = [azr_hi[f] for f in range(6)]
    lo_terms = face_terms(
        from_lo[:5], own_lo[:5], jnp.maximum(from_lo[5], own_lo[5]), (-sin[4], cos[4])
    )
    hi_terms = face_terms(
        own_hi[:5], from_hi[:5], jnp.maximum(from_hi[5], own_hi[5]), (-sin[5], cos[5])
    )
    for f in range(5):
        for a in range(4):
            fix = float(SC[a]) * lo_terms[0][f] + float(SE[a]) * hi_terms[0][f]
            r0[f, 8 * a : 8 * a + 8] = r0[f, 8 * a : 8 * a + 8] - k_a * fix
        aface[f] = k_a * lo_terms[1][f]
        aface[5 + f] = k_a * lo_terms[2][f]
        aface[10 + f] = k_a * hi_terms[1][f]
        aface[15 + f] = k_a * hi_terms[2][f]

    @pl.when(ax > 0)
    def _():
        arrived(axr_lo, 6)
        pl.when(on_odd_core)(push_axial_down)

    @pl.when(ax == 0)
    def _():
        for f in range(6):
            axr_lo[f] = jnp.full((8, 128), (*FREE, 1.5)[f], F32)

    @pl.when(ax < AXIAL - 1)
    def _():
        arrived(axr_hi, 5)
        pl.when(on_odd_core)(push_axial_up)

    @pl.when(ax == AXIAL - 1)
    def _():
        for f in range(6):
            axr_hi[f] = jnp.full((8, 128), (*FREE, 1.5)[f], F32)

    def spread(ref, f, first):
        got = ref[f]
        return jnp.concatenate(
            [jnp.broadcast_to(got[first + a : first + a + 1], (8, 128)) for a in range(4)], axis=0
        )

    minus, plus = [], []
    for f in range(6):
        if f < 5:
            low, up = (ax_tr[32 * i : 32 * i + 32, 128 * f : 128 * f + 128] for i in range(2))
        else:
            low, up = ax_sp[0:32], ax_sp[32:64]
        minus.append(jnp.where(sub32 < 3, spread(axr_lo, f, 4), up))
        plus.append(jnp.where(sub32 == 3, spread(axr_hi, f, 0), low))
    terms = face_terms(minus[:5], plus[:5], jnp.maximum(minus[5], plus[5]), None)
    fix_z = dot(axm[176:208], jnp.concatenate(terms[0] + terms[1] + terms[2], axis=1))
    for f in range(5):
        r0[f] = r0[f] - k_z * fix_z[:, 128 * f : 128 * f + 128]
        bz[f] = bz[f] + k_z * fix_z[:, 640 + 128 * f : 768 + 128 * f]
        cz[f] = k_z * fix_z[:, 1280 + 128 * f : 1408 + 128 * f]

    arrived(radr, 7)

    @pl.when(ra == 0)
    def _():
        push(rads, radr, 7, {"radial": 1}).start()

    lowest = lane32 < 4
    highest = lane32 == 127
    minus, plus = [], []
    got = radr[...]
    for f in range(6):
        ghost = jnp.broadcast_to(got[:, f : f + 1], (32, 128))
        minus.append(jnp.where(lowest, jnp.where(inner, rad_lo[f], ghost), rad_up[f]))
        free = (*FREE, 1.0)[f]
        plus.append(jnp.where(highest, jnp.where(inner, ghost, free), rad_lo[f]))
    base, mean, half_jump = face_terms(
        minus[:5], plus[:5], jnp.maximum(minus[5], plus[5]), (cos32, sin32)
    )
    at_wall = lowest & inner
    pw = pressure_of(plus[:5])
    wall_base = [0.0, pw * cos32, pw * sin32, 0.0, 0.0]
    wall_mean = [0.0, 0.0, 0.0, 0.0, -pw]
    base = [rf32 * jnp.where(at_wall, w, x) for w, x in zip(wall_base, base)]
    mean = [rf32 * jnp.where(at_wall, w, x) for w, x in zip(wall_mean, mean)]
    half_jump = [rf32 * jnp.where(at_wall, 0.0, x) for x in half_jump]
    fix_r = dot(jnp.concatenate(base + mean + half_jump, axis=0), radm[:, 640:768])
    for f in range(5):
        r0[f] = r0[f] - k_r * fix_r[32 * f : 32 * f + 32]
        br[f] = br[f] + k_r * fix_r[160 + 32 * f : 192 + 32 * f]
        cr[f] = k_r * fix_r[320 + 32 * f : 352 + 32 * f]

    loads[7].wait()

    @pl.when(is_root)
    def _():
        pl.semaphore_wait(ready_sem, 2 * AXIAL - 1)
        arrived(p2, 1)
        sums = [p2[i] for i in range(8)]
        for i in range(8, 5 * AZIM - 1):
            sums[i % 8] = sums[i % 8] + p2[i]
        while len(sums) > 1:
            sums = [x + y for x, y in zip(sums[0::2], sums[1::2])]
        p3[...] = col[...] + sums[0]
        for k in (2, 3, 0):
            push(p3, p3, 2, {"axial": k}).start()

    @pl.when(jnp.logical_not(is_root))
    def _():
        arrived(p3, 2)

    @pl.when(is_relay)
    def _():
        for k in (4, 5, 6, 7):
            push(p3, p3, 2, {"axial": k}).start()
        for k in range(AXIAL):
            push(p3, p3, 2, {"axial": k, "radial": 1}).start()

    total = p3[...]
    load = [jnp.broadcast_to(total[:, i : i + 1], (8, 128)) for i in range(4)]
    v = [body_s[0, i] for i in range(3)]
    om = [body_s[0, 3 + i] for i in range(3)]
    spin = [om[0], om[1], 0.25 * om[2]]
    gyro = [
        om[1] * spin[2] - om[2] * spin[1],
        om[2] * spin[0] - om[0] * spin[2],
        om[0] * spin[1] - om[1] * spin[0],
    ]
    v0 = v[0] + 60.0 * load[0]
    v1 = v[1] + 60.0 * load[1]
    v2 = jnp.full((8, 128), v[2], F32)
    o0 = om[0] + 30.0 * (load[2] - gyro[0])
    o1 = om[1] + 30.0 * (load[3] - gyro[1])
    o2 = jnp.full((8, 128), om[2] - 120.0 * gyro[2], F32)
    body_row = zero
    for i, value in enumerate((v0, v1, v2, o0, o1, o2)):
        body_row = jnp.where(lane == i, value, body_row)
    body_ref[...] = body_row[0:1, 0:6]

    along_x = v0 + z * o1
    along_y = v1 - z * o0
    swirl = o2 * r

    def azim_speed(k):
        return cos[k] * along_y - sin[k] * along_x + swirl

    s_a = [azim_speed(k) for k in range(4)]
    s_lo, s_hi = azim_speed(4), azim_speed(5)
    s_r = [cos[a] * along_x + sin[a] * along_y for a in range(4)]
    s_z = [v2 + r * (o0 * sin[a] - o1 * cos[a]) for a in range(4)]
    d0, d1, d2 = DT * o0, DT * o1, DT * o2
    for f in range(5):
        carried = [k_a * s_a[k] * u_v[f, k] for k in range(4)]
        at_lo = s_lo * aface[f] + jnp.abs(s_lo) * aface[5 + f]
        at_hi = s_hi * aface[10 + f] + jnp.abs(s_hi) * aface[15 + f]
        for a in range(4):
            row = slice(8 * a, 8 * a + 8)
            value = r0[f, row] + s_r[a] * br[f, row] + jnp.abs(s_r[a]) * cr[f, row]
            value = value + s_z[a] * bz[f, row] + jnp.abs(s_z[a]) * cz[f, row]
            value = value + weighed(MIX[a], carried)
            value = value + float(SC[a]) * at_lo + float(SE[a]) * at_hi
            if f == 1:
                value = value - (d1 * u_v[3, a] - d2 * u_v[2, a])
            if f == 2:
                value = value - (d2 * u_v[1, a] - d0 * u_v[3, a])
            if f == 3:
                value = value - (d0 * u_v[2, a] - d1 * u_v[1, a])
            out_ref[f, a] = value

    @pl.when(is_root)
    def _():
        left(p2.at[pl.ds(0, AZIM - 1)], 1)
        left(p2.at[pl.ds(0, 3)], 2)

    @pl.when(is_relay)
    def _():
        left(p2.at[pl.ds(0, AXIAL + 4)], 2)

    @pl.when(is_far)
    def _():
        left(p2.at[pl.ds(0, AZIM)], 1)

    @pl.when(is_near)
    def _():
        left(own, 0)

    left(azs_lo, 3)
    left(azs_hi, 4)

    @pl.when(ax > 0)
    def _():
        left(axs, 5)

    @pl.when(ax < AXIAL - 1)
    def _():
        left(axs, 6)

    left(rads, 7)


def store_kernel(out_ref, body_ref, rho_h, mom_h, ene_h, body_h, sems):
    copies = [
        pltpu.make_async_copy(src, dst, sems.at[i])
        for i, (src, dst) in enumerate(
            [
                (out_ref.at[pl.ds(1, 3)], mom_h),
                (out_ref.at[0], rho_h),
                (out_ref.at[4], ene_h),
                (body_ref, body_h),
            ]
        )
    ]
    for copy in copies:
        copy.start()
    for copy in copies:
        copy.wait()


def on_device(density, momentum, energy, wall_flags, body_motion):
    block = density.shape
    hbm = pl.BlockSpec(memory_space=pl.ANY)
    vmem = pl.BlockSpec(memory_space=pltpu.VMEM)
    halo = pltpu.VMEM((6, 8, 128), F32)
    part = pltpu.VMEM((5, 32, 128), F32)
    increment, body_row = pl.pallas_call(
        section_kernel,
        out_shape=(pltpu.VMEM((5, *block), F32), pltpu.VMEM((1, 6), F32)),
        in_specs=[hbm] * 8,
        out_specs=(vmem, vmem),
        scratch_shapes=[
            pltpu.VMEM((5, *block), F32),
            pltpu.VMEM((128, 768), F32),
            pltpu.VMEM((208, 32), F32),
            pltpu.SMEM((1, 128), F32),
            pltpu.SMEM((1, 2), jnp.int32),
            pltpu.SMEM((1, 6), F32),
            pltpu.VMEM((1, 128), F32),
            pltpu.VMEM((1, 128), F32),
            pltpu.VMEM((3, 1, 128), F32),
            pltpu.VMEM((5 * AZIM - 1, 1, 128), F32),
            pltpu.VMEM((1, 128), F32),
            *[halo] * 7,
            pltpu.VMEM((32, 128), F32),
            pltpu.VMEM((32, 128), F32),
            *[part] * 5,
            pltpu.VMEM((20, 8, 128), F32),
            pltpu.SemaphoreType.DMA((8,)),
            pltpu.SemaphoreType.DMA((8,)),
            pltpu.SemaphoreType.DMA((8,)),
            pltpu.SemaphoreType.REGULAR,
        ],
        compiler_params=pltpu.CompilerParams(
            collective_id=0, has_side_effects=True
        ),
    )(
        density,
        momentum,
        energy,
        wall_flags,
        body_motion.reshape(1, 6),
        jnp.asarray(radial_matrices()),
        jnp.asarray(axial_matrices()),
        jnp.asarray(angle_table()),
    )
    increment = pltpu.with_memory_space_constraint(increment, pltpu.VMEM)
    body_row = pltpu.with_memory_space_constraint(body_row, pltpu.VMEM)
    rho, mom, ene, body = pl.pallas_call(
        store_kernel,
        out_shape=(
            jax.ShapeDtypeStruct(block, F32),
            jax.ShapeDtypeStruct((3, *block), F32),
            jax.ShapeDtypeStruct(block, F32),
            jax.ShapeDtypeStruct((1, 6), F32),
        ),
        in_specs=[vmem, vmem],
        out_specs=[hbm] * 4,
        scratch_shapes=[pltpu.SemaphoreType.DMA((4,))],
    )(increment, body_row)
    return rho, mom, ene, body.reshape(6)


def solution(mesh):
    return jax.shard_map(
        on_device,
        mesh=mesh,
        in_specs=(
            P("azim", "axial", "radial"),
            P(None, "azim", "axial", "radial"),
            P("azim", "axial", "radial"),
            P("azim", "axial"),
            P(),
        ),
        out_specs=(
            P("azim", "axial", "radial"),
            P(None, "azim", "axial", "radial"),
            P("azim", "axial", "radial"),
            P(),
        ),
        check_vma=False,
    )
```

```python
import math

import jax
import jax.numpy as jnp
import numpy as np
from jax import lax
from jax.experimental import pallas as pl
from jax.experimental.pallas import tpu as pltpu
from jax.sharding import PartitionSpec as P

MESH = pl.DeviceIdType.MESH
F32 = jnp.float32

AZIM, AXIAL, RADIAL = 32, 8, 2
ROOT = 1
EXTRA = 3
STEP_A = 2.0 * math.pi / 32
STEP_Z = 8.0 / 16
STEP_R = 2.0 / 64
DT = 0.05 * min(STEP_R, STEP_Z, STEP_A)
FREE = (1.0, 0.0, 0.0, 0.5, 1.0 / (1.4 * 0.4) + 0.125)


def fr_tables():
    outer_point = np.sqrt(3.0 / 7.0 + 2.0 / 7.0 * np.sqrt(6.0 / 5.0))
    inner_point = np.sqrt(3.0 / 7.0 - 2.0 / 7.0 * np.sqrt(6.0 / 5.0))
    points = np.array([-outer_point, -inner_point, inner_point, outer_point])
    outer_weight = (18.0 - np.sqrt(30.0)) / 36.0
    inner_weight = (18.0 + np.sqrt(30.0)) / 36.0
    weights = np.array([outer_weight, inner_weight, inner_weight, outer_weight])
    bary_weights = np.array(
        [1.0 / np.prod([points[i] - points[j] for j in range(4) if j != i]) for i in range(4)]
    )
    derivative = np.zeros((4, 4))
    for i in range(4):
        for j in range(4):
            if i != j:
                derivative[i, j] = bary_weights[j] / bary_weights[i] / (points[i] - points[j])
        derivative[i, i] = -np.sum(derivative[i])

    def basis_at(location):
        return np.array(
            [
                np.prod(
                    [(location - points[j]) / (points[i] - points[j]) for j in range(4) if j != i]
                )
                for i in range(4)
            ]
        )

    at_lower = basis_at(-1.0)
    at_upper = basis_at(1.0)
    third_slope = 0.5 * (15.0 * points * points - 3.0)
    fourth_slope = 0.5 * (35.0 * points**3 - 15.0 * points)
    slope_left = 0.5 * (fourth_slope - third_slope)
    slope_right = 0.5 * (fourth_slope + third_slope)
    return (points, weights, derivative, at_lower, at_upper, slope_left, slope_right)


X, Q, D, LA, LB, SC, SE = fr_tables()
OFF = (X + 1.0) / 2.0
MIX = D - np.outer(SC, LA) - np.outer(SE, LB)


def radial_matrices():
    low, up, mean_own, mean_below, mix, corr = (np.zeros((128, 128)) for _ in range(6))
    for j in range(128):
        e, k = divmod(j, 4)
        below = 31 if j == 127 else e - 1
        for i in range(4):
            low[4 * e + i, j] = LA[i]
            mean_own[4 * e + i, j] = Q[i] / 2
            mix[4 * e + i, j] = MIX[k, i]
            if below >= 0:
                up[4 * below + i, j] = LB[i]
                mean_below[4 * below + i, j] = Q[i] / 2
        corr[4 * e, j] += SC[k]
        corr[127 if e == 31 else 4 * (e + 1), j] += SE[k]
    return np.concatenate([low, up, mean_own, mean_below, mix, corr], axis=1).astype(np.float32)


def axial_matrices():
    low, up, mean_low, mean_up, mix, corr = (np.zeros((8, 8)) for _ in range(6))
    for j in range(8):
        e, k = divmod(j, 4)
        own = None if j == 3 else e
        below = 1 if j == 3 else (0 if e == 1 else None)
        for i in range(4):
            if own is not None:
                low[j, 4 * own + i] = LA[i]
                mean_low[j, 4 * own + i] = Q[i] / 2
            if below is not None:
                up[j, 4 * below + i] = LB[i]
                mean_up[j, 4 * below + i] = Q[i] / 2
            mix[j, 4 * e + i] = MIX[k, i]
        corr[j, 4 * e] += SC[k]
        corr[j, 4 if e == 0 else 3] += SE[k]
    pack, pack_mean = np.zeros((8, 32)), np.zeros((8, 32))
    for a in range(4):
        for i in range(4):
            pack[a, 8 * a + i] = LA[i]
            pack[4 + a, 8 * a + 4 + i] = LB[i]
            pack_mean[a, 8 * a + i] = Q[i] / 2
            pack_mean[4 + a, 8 * a + 4 + i] = Q[i] / 2
    four = np.eye(4)
    parts = [np.kron(four, low), np.kron(four, up), pack]
    parts += [np.kron(four, mean_low), np.kron(four, mean_up), pack_mean]
    parts += [np.kron(four, mix), np.kron(four, corr)]
    return np.concatenate(parts, axis=0).astype(np.float32)


def angle_table():
    table = np.zeros((32, 128))
    for e in range(32):
        angles = np.array([*(e + OFF), e, e + 1.0]) * STEP_A
        table[e, 0:6] = np.cos(angles)
        table[e, 6:12] = np.sin(angles)
    return table.astype(np.float32)


def dot(a, b):
    return jnp.dot(a, b, precision=lax.Precision.HIGHEST, preferred_element_type=F32)


def weighed(factors, values):
    total = float(factors[0]) * values[0]
    for factor, value in zip(factors[1:], values[1:]):
        total = total + float(factor) * value
    return total


def pressure_of(u):
    return 0.4 * (u[4] - 0.5 * (u[1] * u[1] + u[2] * u[2] + u[3] * u[3]) / u[0])


def still_flux(u, normal):
    p = pressure_of(u)
    through = u[3] if normal is None else u[1] * normal[0] + u[2] * normal[1]
    vn = through / u[0]
    flux = [through, u[1] * vn, u[2] * vn, u[3] * vn, (u[4] + p) * vn]
    if normal is None:
        flux[3] = flux[3] + p
    else:
        flux[1] = flux[1] + p * normal[0]
        flux[2] = flux[2] + p * normal[1]
    return flux


def face_terms(minus, plus, bound, normal):
    low, high = still_flux(minus, normal), still_flux(plus, normal)
    half_jump = [0.5 * (b - a) for a, b in zip(minus, plus)]
    mean = [0.5 * (a + b) for a, b in zip(minus, plus)]
    base = [0.5 * (a + b) - bound * h for a, b, h in zip(low, high, half_jump)]
    return base, mean, half_jump


def section_kernel(
    rho_h, mom_h, ene_h, flag_h, body_h, radm_h, axm_h, ang_h,
    out_ref, body_ref,
    u_v, radm, axm, ang_s, flag_s, body_s,
    own, col, p1, p2a, p2b, p3,
    azs_lo, azs_hi, azr_lo, azr_hi, axs, axr_lo, axr_hi, rads, radr,
    r0, br, cr, bz, cz, aface,
    load_sem, send_sem, recv_sem, ready_sem,
):
    az, ax, ra = lax.axis_index("azim"), lax.axis_index("axial"), lax.axis_index("radial")
    is_root = (ra == 0) & (ax == ROOT)
    is_near = (ra == 0) & (ax < 4) & (ax != ROOT)
    first_column = az == 0
    is_extra = first_column & (ra == 0) & (ax == EXTRA)
    is_teller = is_extra | (is_root & jnp.logical_not(first_column))
    is_far = (ra == 0) & (ax >= 4)
    is_even = lax.rem(az, 2) == 0
    on_odd_core = lax.rem(ax, 2) == 1
    column_root = {"axial": ROOT, "radial": 0}
    column_teller = {"axial": jnp.where(first_column, EXTRA, ROOT), "radial": 0}
    extra = {"azim": 0, "axial": EXTRA, "radial": 0}

    loads = [
        pltpu.make_async_copy(src, dst, load_sem.at[i])
        for i, (src, dst) in enumerate(
            [
                (ang_h.at[pl.ds(az, 1)], ang_s),
                (flag_h, flag_s),
                (rho_h, u_v.at[0]),
                (mom_h, u_v.at[pl.ds(1, 3)]),
                (ene_h, u_v.at[4]),
                (radm_h, radm),
                (axm_h, axm),
                (body_h, body_s),
            ]
        )
    ]
    for load in loads:
        load.start()

    barrier = pltpu.get_barrier_semaphore()

    def greet(device):
        pl.semaphore_signal(barrier, inc=1, device_id=device, device_id_type=MESH)

    @pl.when(is_root | is_extra)
    def _():
        def greet_column(i, carry):
            for k in (7, 6, 5, 4):
                greet({"azim": i, "axial": k, "radial": 0})
            return carry

        lax.fori_loop(0, AZIM, greet_column, 0)

    @pl.when(is_root)
    def _():
        def greet_root(i, carry):
            greet({"azim": lax.rem(az + i, AZIM)})
            return carry

        lax.fori_loop(1, AZIM, greet_root, 0)
        for k in (0, 2, 3):
            greet({"axial": k})

    @pl.when(is_extra)
    def _():
        def greet_root(i, carry):
            greet({"azim": i, "axial": ROOT})
            return carry

        lax.fori_loop(0, AZIM, greet_root, 0)
        for k in (0, 2):
            greet({"axial": k})

    @pl.when(is_teller)
    def _():
        for k in range(AXIAL):
            greet({"axial": k, "radial": 1})

    below = lax.rem(az + (AZIM - 1), AZIM)
    above = lax.rem(az + 1, AZIM)
    @pl.when(is_even)
    def _():
        greet({"azim": below})
        greet({"azim": above})

    @pl.when(on_odd_core)
    def _():
        greet({"axial": ax - 1})

    @pl.when(on_odd_core & (ax < AXIAL - 1))
    def _():
        greet({"axial": ax + 1})

    @pl.when(ra == 0)
    def _():
        greet({"radial": 1})

    sub = lax.broadcasted_iota(jnp.int32, (8, 128), 0)
    lane = lax.broadcasted_iota(jnp.int32, (8, 128), 1)
    lane32 = lax.broadcasted_iota(jnp.int32, (32, 128), 1)
    sub32 = lax.broadcasted_iota(jnp.int32, (32, 128), 0) & 7

    def by_place(place, values):
        out = jnp.full(place.shape, float(values[3]), F32)
        for k in range(3):
            out = jnp.where(place == k, float(values[k]), out)
        return out

    z = ((ax * 2 + (sub >> 2)).astype(F32) + by_place(sub & 3, OFF)) * STEP_Z
    elem_r = (ra * 32 + (lane >> 2)).astype(F32)
    r = 1.0 + (elem_r + by_place(lane & 3, OFF)) * STEP_R
    r_face = 1.0 + (elem_r + jnp.where(lane == 127, 1.0, 0.0)) * STEP_R

    loads[0].wait()
    loads[1].wait()
    cos = [ang_s[0, k] for k in range(6)]
    sin = [ang_s[0, 6 + k] for k in range(6)]
    flag = jnp.where(
        sub < 4,
        jnp.full((8, 128), flag_s[0, 0], jnp.int32),
        jnp.full((8, 128), flag_s[0, 1], jnp.int32),
    ).astype(F32)
    area_z = flag * by_place(sub & 3, Q * (0.5 * STEP_Z))
    zero = jnp.zeros((8, 128), F32)
    load_w = []
    for a in range(4):
        arm = jnp.where(lane >= 2, z, 1.0) * area_z * float(Q[a] * (0.5 * STEP_A))
        turn = jnp.where((lane == 0) | (lane == 3), -cos[a], jnp.where(lane == 1, -sin[a], sin[a]))
        load_w.append(jnp.where(lane < 4, arm * turn, zero))
    load_w = jnp.concatenate(load_w, axis=0)
    wall_a = jnp.where(lane32 < 4, by_place(lane32 & 3, LA), 0.0)
    loads[2].wait()
    loads[3].wait()
    loads[4].wait()
    u = [u_v[f].reshape(32, 128) for f in range(5)]

    wall = [jnp.sum(x * wall_a, axis=1, keepdims=True) for x in u]
    own[...] = jnp.sum(pressure_of(wall) * load_w, axis=0, keepdims=True)

    by_column = jnp.where(first_column & (ax != EXTRA), 2, 1)
    greeted = jnp.where(is_even, 0, 2)
    greeted = greeted + jnp.where(on_odd_core, 0, jnp.where(ax > 0, 2, 1))
    greeted = greeted + jnp.where(
        ra == 1, 2, jnp.where(ax == ROOT, AZIM, jnp.where(ax >= 4, AZIM + 1, by_column))
    )
    pl.semaphore_wait(barrier, greeted)

    def push(src, dst, lane_of, device):
        return pltpu.make_async_remote_copy(
            src_ref=src,
            dst_ref=dst,
            send_sem=send_sem.at[lane_of],
            recv_sem=recv_sem.at[lane_of],
            device_id=device,
            device_id_type=MESH,
        )

    def arrived(ref, lane_of):
        pltpu.make_async_copy(ref, ref, recv_sem.at[lane_of]).wait()

    def left(ref, lane_of):
        pltpu.make_async_copy(ref, ref, send_sem.at[lane_of]).wait()

    def tell_all(src, dst, lane_of, first):
        def send(i, carry):
            push(src, dst, lane_of, {"azim": lax.rem(az + i, AZIM), "axial": ROOT, "radial": 0}).start()
            return carry

        def send_direct(i, carry):
            push(src, dst, lane_of, {"azim": i, "axial": ROOT, "radial": 0}).start()
            return carry

        if first:
            push(src, dst, lane_of, extra).start()
            lax.fori_loop(1, AZIM, send, 0)
        else:
            send_direct(0, 0)
            push(src, dst, lane_of, extra).start()
            lax.fori_loop(1, AZIM, send_direct, 0)

    @pl.when(is_far & (ax >= 6))
    def _():
        tell_all(own, p2a.at[az * 2 + (ax - 6)], 1, False)

    @pl.when(is_far & (ax < 6))
    def _():
        tell_all(own, p2b.at[az * 2 + (ax - 4)], 8, False)

    @pl.when(is_near)
    def _():
        push(own, p1.at[jnp.where(ax == 0, 0, ax - 1)], 0, column_root).start()

    is_told = jnp.logical_not(is_root | is_extra)

    @pl.when(is_told)
    def _():
        pl.semaphore_signal(ready_sem, inc=1, device_id=column_teller, device_id_type=MESH)

    rho = u[0]
    p = pressure_of(u)
    sound = jnp.sqrt(1.4 * p / rho)
    cos32 = jnp.concatenate([jnp.full((8, 128), cos[a], F32) for a in range(4)], axis=0)
    sin32 = jnp.concatenate([jnp.full((8, 128), sin[a], F32) for a in range(4)], axis=0)
    speed_r = jnp.abs((u[1] * cos32 + u[2] * sin32) / rho) + sound
    speed_a = jnp.abs((u[2] * cos32 - u[1] * sin32) / rho) + sound
    speed_z = jnp.abs(u[3] / rho) + sound

    def rows(x):
        return [x[8 * a : 8 * a + 8] for a in range(4)]

    u_rows = [rows(x) for x in u]
    mean_a = weighed(Q / 2, rows(speed_a))
    for f in range(5):
        azs_lo[f] = weighed(LA, u_rows[f])
        azs_hi[f] = weighed(LB, u_rows[f])
    azs_lo[5] = mean_a
    azs_hi[5] = mean_a

    def push_azim():
        push(azs_lo, azr_hi, 3, {"azim": below}).start()
        push(azs_hi, azr_lo, 4, {"azim": above}).start()

    pl.when(jnp.logical_not(is_even))(push_azim)

    loads[5].wait()
    loads[6].wait()
    u_wide = jnp.concatenate(u, axis=1)
    ax_tr = dot(axm[0:72], u_wide)
    ax_sp = dot(axm[72:144], speed_z)
    for f in range(5):
        axs[f] = ax_tr[64:72, 128 * f : 128 * (f + 1)]
    axs[5] = ax_sp[64:72]

    def push_axial_down():
        push(axs, axr_hi, 5, {"axial": ax - 1}).start()

    def push_axial_up():
        push(axs, axr_lo, 6, {"axial": ax + 1}).start()

    pl.when(jnp.logical_not(on_odd_core) & (ax > 0))(push_axial_down)
    pl.when(jnp.logical_not(on_odd_core))(push_axial_up)

    rad_tr = dot(jnp.concatenate(u, axis=0), radm[:, 0:256])
    rad_sp = dot(speed_r, radm[:, 256:512])
    rad_lo = [rad_tr[32 * f : 32 * f + 32, 0:128] for f in range(5)] + [rad_sp[:, 0:128]]
    rad_up = [rad_tr[32 * f : 32 * f + 32, 128:256] for f in range(5)] + [rad_sp[:, 128:256]]
    inner = jnp.full((32, 128), ra, jnp.int32) == 0
    packed = jnp.zeros((32, 128), F32)
    for f in range(6):
        edge = jnp.where(
            inner,
            jnp.broadcast_to(rad_up[f][:, 127:128], (32, 128)),
            jnp.broadcast_to(rad_lo[f][:, 0:1], (32, 128)),
        )
        packed = jnp.where(lane32 == f, edge, packed)
    rads[...] = packed

    @pl.when(ra == 1)
    def _():
        push(rads, radr, 7, {"radial": 0}).start()

    @pl.when(is_root)
    def _():
        arrived(p1, 0)
        col[...] = own[...] + jnp.sum(p1[...], axis=0)
        p2b[2 * AZIM + az] = col[...]
        tell_all(col, p2b.at[2 * AZIM + az], 8, True)

    r32 = jnp.concatenate([r] * 4, axis=0)
    rf32 = jnp.concatenate([r_face] * 4, axis=0)
    k_r = (DT * 2.0 / STEP_R) / r32
    k_a = (DT * 2.0 / STEP_A) / r
    k_a32 = jnp.concatenate([k_a] * 4, axis=0)
    k_z = DT * 2.0 / STEP_Z
    flux_r = still_flux(u, (cos32, sin32))
    flux_a = still_flux(u, (-sin32, cos32))
    flux_z = still_flux(u, None)
    mix_r = dot(
        jnp.concatenate([r32 * x for x in flux_r] + [r32 * x for x in u], axis=0), radm[:, 512:640]
    )
    mix_z = dot(axm[144:176], jnp.concatenate(flux_z + u, axis=1))
    for f in range(5):
        flux_rows = rows(flux_a[f])
        mix_a = jnp.concatenate([weighed(MIX[a], flux_rows) for a in range(4)], axis=0)
        r0[f] = (
            -k_r * mix_r[32 * f : 32 * f + 32]
            - k_a32 * mix_a
            - k_z * mix_z[:, 128 * f : 128 * f + 128]
        )
        br[f] = k_r * mix_r[160 + 32 * f : 192 + 32 * f]
        bz[f] = k_z * mix_z[:, 640 + 128 * f : 768 + 128 * f]

    arrived(azr_lo, 4)
    arrived(azr_hi, 3)
    pl.when(is_even)(push_azim)
    own_lo = [azs_lo[f] for f in range(6)]
    own_hi = [azs_hi[f] for f in range(6)]
    from_lo = [azr_lo[f] for f in range(6)]
    from_hi = [azr_hi[f] for f in range(6)]
    lo_terms = face_terms(
        from_lo[:5], own_lo[:5], jnp.maximum(from_lo[5], own_lo[5]), (-sin[4], cos[4])
    )
    hi_terms = face_terms(
        own_hi[:5], from_hi[:5], jnp.maximum(from_hi[5], own_hi[5]), (-sin[5], cos[5])
    )
    for f in range(5):
        for a in range(4):
            fix = float(SC[a]) * lo_terms[0][f] + float(SE[a]) * hi_terms[0][f]
            r0[f, 8 * a : 8 * a + 8] = r0[f, 8 * a : 8 * a + 8] - k_a * fix
        aface[f] = k_a * lo_terms[1][f]
        aface[5 + f] = k_a * lo_terms[2][f]
        aface[10 + f] = k_a * hi_terms[1][f]
        aface[15 + f] = k_a * hi_terms[2][f]

    @pl.when(ax > 0)
    def _():
        arrived(axr_lo, 6)
        pl.when(on_odd_core)(push_axial_down)

    @pl.when(ax == 0)
    def _():
        for f in range(6):
            axr_lo[f] = jnp.full((8, 128), (*FREE, 1.5)[f], F32)

    @pl.when(ax < AXIAL - 1)
    def _():
        arrived(axr_hi, 5)
        pl.when(on_odd_core)(push_axial_up)

    @pl.when(ax == AXIAL - 1)
    def _():
        for f in range(6):
            axr_hi[f] = jnp.full((8, 128), (*FREE, 1.5)[f], F32)

    def spread(ref, f, first):
        got = ref[f]
        return jnp.concatenate(
            [jnp.broadcast_to(got[first + a : first + a + 1], (8, 128)) for a in range(4)], axis=0
        )

    minus, plus = [], []
    for f in range(6):
        if f < 5:
            low, up = (ax_tr[32 * i : 32 * i + 32, 128 * f : 128 * f + 128] for i in range(2))
        else:
            low, up = ax_sp[0:32], ax_sp[32:64]
        minus.append(jnp.where(sub32 < 3, spread(axr_lo, f, 4), up))
        plus.append(jnp.where(sub32 == 3, spread(axr_hi, f, 0), low))
    terms = face_terms(minus[:5], plus[:5], jnp.maximum(minus[5], plus[5]), None)
    fix_z = dot(axm[176:208], jnp.concatenate(terms[0] + terms[1] + terms[2], axis=1))
    for f in range(5):
        r0[f] = r0[f] - k_z * fix_z[:, 128 * f : 128 * f + 128]
        bz[f] = bz[f] + k_z * fix_z[:, 640 + 128 * f : 768 + 128 * f]
        cz[f] = k_z * fix_z[:, 1280 + 128 * f : 1408 + 128 * f]

    arrived(radr, 7)

    @pl.when(ra == 0)
    def _():
        push(rads, radr, 7, {"radial": 1}).start()

    lowest = lane32 < 4
    highest = lane32 == 127
    minus, plus = [], []
    got = radr[...]
    for f in range(6):
        ghost = jnp.broadcast_to(got[:, f : f + 1], (32, 128))
        minus.append(jnp.where(lowest, jnp.where(inner, rad_lo[f], ghost), rad_up[f]))
        free = (*FREE, 1.0)[f]
        plus.append(jnp.where(highest, jnp.where(inner, ghost, free), rad_lo[f]))
    base, mean, half_jump = face_terms(
        minus[:5], plus[:5], jnp.maximum(minus[5], plus[5]), (cos32, sin32)
    )
    at_wall = lowest & inner
    pw = pressure_of(plus[:5])
    wall_base = [0.0, pw * cos32, pw * sin32, 0.0, 0.0]
    wall_mean = [0.0, 0.0, 0.0, 0.0, -pw]
    base = [rf32 * jnp.where(at_wall, w, x) for w, x in zip(wall_base, base)]
    mean = [rf32 * jnp.where(at_wall, w, x) for w, x in zip(wall_mean, mean)]
    half_jump = [rf32 * jnp.where(at_wall, 0.0, x) for x in half_jump]
    fix_r = dot(jnp.concatenate(base + mean + half_jump, axis=0), radm[:, 640:768])
    for f in range(5):
        r0[f] = r0[f] - k_r * fix_r[32 * f : 32 * f + 32]
        br[f] = br[f] + k_r * fix_r[160 + 32 * f : 192 + 32 * f]
        cr[f] = k_r * fix_r[320 + 32 * f : 352 + 32 * f]

    loads[7].wait()

    @pl.when(is_root)
    def _():
        arrived(p2b.at[pl.ds(0, 3 * AZIM - 1)], 8)

    @pl.when(is_extra)
    def _():
        arrived(p2b, 8)

    @pl.when(is_extra)
    def _():
        pl.semaphore_wait(ready_sem, 2 * AXIAL - 2)

    @pl.when(is_teller & is_root)
    def _():
        pl.semaphore_wait(ready_sem, 2 * AXIAL - 1)

    def sum_rows(ref, count):
        sums = [ref[i] for i in range(8)]
        for i in range(8, count):
            sums[i % 8] = sums[i % 8] + ref[i]
        while len(sums) > 1:
            sums = [x + y for x, y in zip(sums[0::2], sums[1::2])]
        return sums[0]

    @pl.when(is_root | is_extra)
    def _():
        early = sum_rows(p2b, 3 * AZIM)
        arrived(p2a, 1)
        p3[...] = early + sum_rows(p2a, 2 * AZIM)

    @pl.when(is_teller)
    def _():
        @pl.when(is_root)
        def _():
            push(p3, p3, 2, {"axial": EXTRA}).start()

        for k in (2, 0, 4, 5, 6, 7):
            push(p3, p3, 2, {"axial": k}).start()
        for k in range(AXIAL):
            push(p3, p3, 2, {"axial": k, "radial": 1}).start()

    @pl.when(is_told)
    def _():
        arrived(p3, 2)

    total = p3[...]
    load = [jnp.broadcast_to(total[:, i : i + 1], (8, 128)) for i in range(4)]
    v = [body_s[0, i] for i in range(3)]
    om = [body_s[0, 3 + i] for i in range(3)]
    spin = [om[0], om[1], 0.25 * om[2]]
    gyro = [
        om[1] * spin[2] - om[2] * spin[1],
        om[2] * spin[0] - om[0] * spin[2],
        om[0] * spin[1] - om[1] * spin[0],
    ]
    v0 = v[0] + 60.0 * load[0]
    v1 = v[1] + 60.0 * load[1]
    v2 = jnp.full((8, 128), v[2], F32)
    o0 = om[0] + 30.0 * (load[2] - gyro[0])
    o1 = om[1] + 30.0 * (load[3] - gyro[1])
    o2 = jnp.full((8, 128), om[2] - 120.0 * gyro[2], F32)
    body_row = zero
    for i, value in enumerate((v0, v1, v2, o0, o1, o2)):
        body_row = jnp.where(lane == i, value, body_row)
    body_ref[...] = body_row[0:1, 0:6]

    along_x = v0 + z * o1
    along_y = v1 - z * o0
    swirl = o2 * r

    def azim_speed(k):
        return cos[k] * along_y - sin[k] * along_x + swirl

    s_a = [azim_speed(k) for k in range(4)]
    s_lo, s_hi = azim_speed(4), azim_speed(5)
    s_r = [cos[a] * along_x + sin[a] * along_y for a in range(4)]
    s_z = [v2 + r * (o0 * sin[a] - o1 * cos[a]) for a in range(4)]
    d0, d1, d2 = DT * o0, DT * o1, DT * o2
    for f in range(5):
        carried = [k_a * s_a[k] * u_v[f, k] for k in range(4)]
        at_lo = s_lo * aface[f] + jnp.abs(s_lo) * aface[5 + f]
        at_hi = s_hi * aface[10 + f] + jnp.abs(s_hi) * aface[15 + f]
        for a in range(4):
            row = slice(8 * a, 8 * a + 8)
            value = r0[f, row] + s_r[a] * br[f, row] + jnp.abs(s_r[a]) * cr[f, row]
            value = value + s_z[a] * bz[f, row] + jnp.abs(s_z[a]) * cz[f, row]
            value = value + weighed(MIX[a], carried)
            value = value + float(SC[a]) * at_lo + float(SE[a]) * at_hi
            if f == 1:
                value = value - (d1 * u_v[3, a] - d2 * u_v[2, a])
            if f == 2:
                value = value - (d2 * u_v[1, a] - d0 * u_v[3, a])
            if f == 3:
                value = value - (d0 * u_v[2, a] - d1 * u_v[1, a])
            out_ref[f, a] = value

    @pl.when(is_root)
    def _():
        left(p2b.at[pl.ds(0, AZIM)], 8)

    @pl.when(is_teller & is_root)
    def _():
        left(p2b.at[pl.ds(0, 2 * AXIAL - 1)], 2)

    @pl.when(is_extra)
    def _():
        left(p2b.at[pl.ds(0, 2 * AXIAL - 2)], 2)

    @pl.when(is_far & (ax >= 6))
    def _():
        left(p2b.at[pl.ds(0, AZIM + 1)], 1)

    @pl.when(is_far & (ax < 6))
    def _():
        left(p2b.at[pl.ds(0, AZIM + 1)], 8)

    @pl.when(is_near)
    def _():
        left(own, 0)

    left(azs_lo, 3)
    left(azs_hi, 4)

    @pl.when(ax > 0)
    def _():
        left(axs, 5)

    @pl.when(ax < AXIAL - 1)
    def _():
        left(axs, 6)

    left(rads, 7)


def store_kernel(out_ref, body_ref, rho_h, mom_h, ene_h, body_h, sems):
    copies = [
        pltpu.make_async_copy(src, dst, sems.at[i])
        for i, (src, dst) in enumerate(
            [
                (out_ref.at[pl.ds(1, 3)], mom_h),
                (out_ref.at[0], rho_h),
                (out_ref.at[4], ene_h),
                (body_ref, body_h),
            ]
        )
    ]
    for copy in copies:
        copy.start()
    for copy in copies:
        copy.wait()


def on_device(density, momentum, energy, wall_flags, body_motion):
    block = density.shape
    hbm = pl.BlockSpec(memory_space=pl.ANY)
    vmem = pl.BlockSpec(memory_space=pltpu.VMEM)
    halo = pltpu.VMEM((6, 8, 128), F32)
    part = pltpu.VMEM((5, 32, 128), F32)
    increment, body_row = pl.pallas_call(
        section_kernel,
        out_shape=(pltpu.VMEM((5, *block), F32), pltpu.VMEM((1, 6), F32)),
        in_specs=[hbm] * 8,
        out_specs=(vmem, vmem),
        scratch_shapes=[
            pltpu.VMEM((5, *block), F32),
            pltpu.VMEM((128, 768), F32),
            pltpu.VMEM((208, 32), F32),
            pltpu.SMEM((1, 128), F32),
            pltpu.SMEM((1, 2), jnp.int32),
            pltpu.SMEM((1, 6), F32),
            pltpu.VMEM((1, 128), F32),
            pltpu.VMEM((1, 128), F32),
            pltpu.VMEM((3, 1, 128), F32),
            pltpu.VMEM((2 * AZIM, 1, 128), F32),
            pltpu.VMEM((3 * AZIM, 1, 128), F32),
            pltpu.VMEM((1, 128), F32),
            *[halo] * 7,
            pltpu.VMEM((32, 128), F32),
            pltpu.VMEM((32, 128), F32),
            *[part] * 5,
            pltpu.VMEM((20, 8, 128), F32),
            pltpu.SemaphoreType.DMA((8,)),
            pltpu.SemaphoreType.DMA((9,)),
            pltpu.SemaphoreType.DMA((9,)),
            pltpu.SemaphoreType.REGULAR,
        ],
        compiler_params=pltpu.CompilerParams(
            collective_id=0, has_side_effects=True
        ),
    )(
        density,
        momentum,
        energy,
        wall_flags,
        body_motion.reshape(1, 6),
        jnp.asarray(radial_matrices()),
        jnp.asarray(axial_matrices()),
        jnp.asarray(angle_table()),
    )
    increment = pltpu.with_memory_space_constraint(increment, pltpu.VMEM)
    body_row = pltpu.with_memory_space_constraint(body_row, pltpu.VMEM)
    rho, mom, ene, body = pl.pallas_call(
        store_kernel,
        out_shape=(
            jax.ShapeDtypeStruct(block, F32),
            jax.ShapeDtypeStruct((3, *block), F32),
            jax.ShapeDtypeStruct(block, F32),
            jax.ShapeDtypeStruct((1, 6), F32),
        ),
        in_specs=[vmem, vmem],
        out_specs=[hbm] * 4,
        scratch_shapes=[pltpu.SemaphoreType.DMA((4,))],
    )(increment, body_row)
    return rho, mom, ene, body.reshape(6)


def solution(mesh):
    return jax.shard_map(
        on_device,
        mesh=mesh,
        in_specs=(
            P("azim", "axial", "radial"),
            P(None, "azim", "axial", "radial"),
            P("azim", "axial", "radial"),
            P("azim", "axial"),
            P(),
        ),
        out_specs=(
            P("azim", "axial", "radial"),
            P(None, "azim", "axial", "radial"),
            P("azim", "axial", "radial"),
            P(),
        ),
        check_vma=False,
    )
```

```python
import math

import jax
import jax.numpy as jnp
import numpy as np
from jax import lax
from jax.experimental import pallas as pl
from jax.experimental.pallas import tpu as pltpu
from jax.sharding import PartitionSpec as P

MESH = pl.DeviceIdType.MESH
F32 = jnp.float32

AZIM, AXIAL, RADIAL = 32, 8, 2
ROOT = 1
EXTRA = 3
STEP_A = 2.0 * math.pi / 32
STEP_Z = 8.0 / 16
STEP_R = 2.0 / 64
DT = 0.05 * min(STEP_R, STEP_Z, STEP_A)
FREE = (1.0, 0.0, 0.0, 0.5, 1.0 / (1.4 * 0.4) + 0.125)


def fr_tables():
    outer_point = np.sqrt(3.0 / 7.0 + 2.0 / 7.0 * np.sqrt(6.0 / 5.0))
    inner_point = np.sqrt(3.0 / 7.0 - 2.0 / 7.0 * np.sqrt(6.0 / 5.0))
    points = np.array([-outer_point, -inner_point, inner_point, outer_point])
    outer_weight = (18.0 - np.sqrt(30.0)) / 36.0
    inner_weight = (18.0 + np.sqrt(30.0)) / 36.0
    weights = np.array([outer_weight, inner_weight, inner_weight, outer_weight])
    bary_weights = np.array(
        [1.0 / np.prod([points[i] - points[j] for j in range(4) if j != i]) for i in range(4)]
    )
    derivative = np.zeros((4, 4))
    for i in range(4):
        for j in range(4):
            if i != j:
                derivative[i, j] = bary_weights[j] / bary_weights[i] / (points[i] - points[j])
        derivative[i, i] = -np.sum(derivative[i])

    def basis_at(location):
        return np.array(
            [
                np.prod(
                    [(location - points[j]) / (points[i] - points[j]) for j in range(4) if j != i]
                )
                for i in range(4)
            ]
        )

    at_lower = basis_at(-1.0)
    at_upper = basis_at(1.0)
    third_slope = 0.5 * (15.0 * points * points - 3.0)
    fourth_slope = 0.5 * (35.0 * points**3 - 15.0 * points)
    slope_left = 0.5 * (fourth_slope - third_slope)
    slope_right = 0.5 * (fourth_slope + third_slope)
    return (points, weights, derivative, at_lower, at_upper, slope_left, slope_right)


X, Q, D, LA, LB, SC, SE = fr_tables()
OFF = (X + 1.0) / 2.0
MIX = D - np.outer(SC, LA) - np.outer(SE, LB)


def radial_matrices():
    low, up, mean_own, mean_below, mix, corr = (np.zeros((128, 128)) for _ in range(6))
    for j in range(128):
        e, k = divmod(j, 4)
        below = 31 if j == 127 else e - 1
        for i in range(4):
            low[4 * e + i, j] = LA[i]
            mean_own[4 * e + i, j] = Q[i] / 2
            mix[4 * e + i, j] = MIX[k, i]
            if below >= 0:
                up[4 * below + i, j] = LB[i]
                mean_below[4 * below + i, j] = Q[i] / 2
        corr[4 * e, j] += SC[k]
        corr[127 if e == 31 else 4 * (e + 1), j] += SE[k]
    return np.concatenate([low, up, mean_own, mean_below, mix, corr], axis=1).astype(np.float32)


def axial_matrices():
    low, up, mean_low, mean_up, mix, corr = (np.zeros((8, 8)) for _ in range(6))
    for j in range(8):
        e, k = divmod(j, 4)
        own = None if j == 3 else e
        below = 1 if j == 3 else (0 if e == 1 else None)
        for i in range(4):
            if own is not None:
                low[j, 4 * own + i] = LA[i]
                mean_low[j, 4 * own + i] = Q[i] / 2
            if below is not None:
                up[j, 4 * below + i] = LB[i]
                mean_up[j, 4 * below + i] = Q[i] / 2
            mix[j, 4 * e + i] = MIX[k, i]
        corr[j, 4 * e] += SC[k]
        corr[j, 4 if e == 0 else 3] += SE[k]
    pack, pack_mean = np.zeros((8, 32)), np.zeros((8, 32))
    for a in range(4):
        for i in range(4):
            pack[a, 8 * a + i] = LA[i]
            pack[4 + a, 8 * a + 4 + i] = LB[i]
            pack_mean[a, 8 * a + i] = Q[i] / 2
            pack_mean[4 + a, 8 * a + 4 + i] = Q[i] / 2
    four = np.eye(4)
    parts = [np.kron(four, low), np.kron(four, up), pack]
    parts += [np.kron(four, mean_low), np.kron(four, mean_up), pack_mean]
    parts += [np.kron(four, mix), np.kron(four, corr)]
    return np.concatenate(parts, axis=0).astype(np.float32)


def angle_table():
    table = np.zeros((32, 128))
    for e in range(32):
        angles = np.array([*(e + OFF), e, e + 1.0]) * STEP_A
        table[e, 0:6] = np.cos(angles)
        table[e, 6:12] = np.sin(angles)
    return table.astype(np.float32)


def dot(a, b):
    return jnp.dot(a, b, precision=lax.Precision.HIGHEST, preferred_element_type=F32)


def weighed(factors, values):
    total = float(factors[0]) * values[0]
    for factor, value in zip(factors[1:], values[1:]):
        total = total + float(factor) * value
    return total


def pressure_of(u):
    return 0.4 * (u[4] - 0.5 * (u[1] * u[1] + u[2] * u[2] + u[3] * u[3]) / u[0])


def still_flux(u, normal):
    p = pressure_of(u)
    through = u[3] if normal is None else u[1] * normal[0] + u[2] * normal[1]
    vn = through / u[0]
    flux = [through, u[1] * vn, u[2] * vn, u[3] * vn, (u[4] + p) * vn]
    if normal is None:
        flux[3] = flux[3] + p
    else:
        flux[1] = flux[1] + p * normal[0]
        flux[2] = flux[2] + p * normal[1]
    return flux


def face_terms(minus, plus, bound, normal):
    low, high = still_flux(minus, normal), still_flux(plus, normal)
    half_jump = [0.5 * (b - a) for a, b in zip(minus, plus)]
    mean = [0.5 * (a + b) for a, b in zip(minus, plus)]
    base = [0.5 * (a + b) - bound * h for a, b, h in zip(low, high, half_jump)]
    return base, mean, half_jump


def section_kernel(
    rho_h, mom_h, ene_h, flag_h, body_h, radm_h, axm_h, ang_h,
    out_ref, body_ref,
    u_v, radm, axm, ang_s, flag_s, body_s,
    own, col, p1, p2a, p2b, p3,
    azs_lo, azs_hi, azr_lo, azr_hi, axs, axr_lo, axr_hi, rads, radr,
    r0, br, cr, bz, cz, aface,
    load_sem, send_sem, recv_sem, ready_sem,
):
    az, ax, ra = lax.axis_index("azim"), lax.axis_index("axial"), lax.axis_index("radial")
    is_root = (ra == 0) & (ax == ROOT)
    is_near = (ra == 0) & (ax < 4) & (ax != ROOT)
    first_column = az == 0
    is_extra = first_column & (ra == 0) & (ax == EXTRA)
    is_teller = is_extra | (is_root & jnp.logical_not(first_column))
    is_far = (ra == 0) & (ax >= 4)
    is_even = lax.rem(az, 2) == 0
    late = (ax == 0) & (ra == 0)
    greets_above = (is_even & jnp.logical_not(late & (az == 0))) | (late & (az == AZIM - 1))
    greets_below = (is_even & jnp.logical_not(late & (az == 0))) | (late & (az == 1))
    on_odd_core = lax.rem(ax, 2) == 1
    column_root = {"axial": ROOT, "radial": 0}
    column_teller = {"axial": jnp.where(first_column, EXTRA, ROOT), "radial": 0}
    extra = {"azim": 0, "axial": EXTRA, "radial": 0}

    loads = [
        pltpu.make_async_copy(src, dst, load_sem.at[i])
        for i, (src, dst) in enumerate(
            [
                (ang_h.at[pl.ds(az, 1)], ang_s),
                (flag_h, flag_s),
                (rho_h, u_v.at[0]),
                (mom_h, u_v.at[pl.ds(1, 3)]),
                (ene_h, u_v.at[4]),
                (radm_h, radm),
                (axm_h, axm),
                (body_h, body_s),
            ]
        )
    ]
    for load in loads:
        load.start()

    barrier = pltpu.get_barrier_semaphore()

    def greet(device):
        pl.semaphore_signal(barrier, inc=1, device_id=device, device_id_type=MESH)

    @pl.when(is_root | is_extra)
    def _():
        def greet_column(i, carry):
            for k in (7, 6, 5, 4):
                greet({"azim": i, "axial": k, "radial": 0})
            return carry

        lax.fori_loop(0, AZIM, greet_column, 0)

    @pl.when(is_root)
    def _():
        def greet_root(i, carry):
            greet({"azim": lax.rem(az + i, AZIM)})
            return carry

        lax.fori_loop(1, AZIM, greet_root, 0)
        for k in (0, 2, 3):
            greet({"axial": k})

    @pl.when(is_extra)
    def _():
        def greet_root(i, carry):
            greet({"azim": i, "axial": ROOT})
            return carry

        lax.fori_loop(0, AZIM, greet_root, 0)
        for k in (0, 2):
            greet({"axial": k})

    @pl.when(is_teller)
    def _():
        for k in range(AXIAL):
            greet({"axial": k, "radial": 1})

    below = lax.rem(az + (AZIM - 1), AZIM)
    above = lax.rem(az + 1, AZIM)
    @pl.when(greets_above)
    def _():
        greet({"azim": above})

    @pl.when(greets_below)
    def _():
        greet({"azim": below})

    @pl.when(on_odd_core)
    def _():
        greet({"axial": ax - 1})

    @pl.when(on_odd_core & (ax < AXIAL - 1))
    def _():
        greet({"axial": ax + 1})

    @pl.when(ra == 0)
    def _():
        greet({"radial": 1})

    sub = lax.broadcasted_iota(jnp.int32, (8, 128), 0)
    lane = lax.broadcasted_iota(jnp.int32, (8, 128), 1)
    lane32 = lax.broadcasted_iota(jnp.int32, (32, 128), 1)
    sub32 = lax.broadcasted_iota(jnp.int32, (32, 128), 0) & 7

    def by_place(place, values):
        out = jnp.full(place.shape, float(values[3]), F32)
        for k in range(3):
            out = jnp.where(place == k, float(values[k]), out)
        return out

    z = ((ax * 2 + (sub >> 2)).astype(F32) + by_place(sub & 3, OFF)) * STEP_Z
    elem_r = (ra * 32 + (lane >> 2)).astype(F32)
    r = 1.0 + (elem_r + by_place(lane & 3, OFF)) * STEP_R
    r_face = 1.0 + (elem_r + jnp.where(lane == 127, 1.0, 0.0)) * STEP_R

    for load in loads[:5]:
        load.wait()
    cos = [ang_s[0, k] for k in range(6)]
    sin = [ang_s[0, 6 + k] for k in range(6)]
    flag = jnp.where(
        sub < 4,
        jnp.full((8, 128), flag_s[0, 0], jnp.int32),
        jnp.full((8, 128), flag_s[0, 1], jnp.int32),
    ).astype(F32)
    area_z = flag * by_place(sub & 3, Q * (0.5 * STEP_Z))
    zero = jnp.zeros((8, 128), F32)
    load_w = []
    for a in range(4):
        arm = jnp.where(lane >= 2, z, 1.0) * area_z * float(Q[a] * (0.5 * STEP_A))
        turn = jnp.where((lane == 0) | (lane == 3), -cos[a], jnp.where(lane == 1, -sin[a], sin[a]))
        load_w.append(jnp.where(lane < 4, arm * turn, zero))
    load_w = jnp.concatenate(load_w, axis=0)
    wall_a = jnp.where(lane32 < 4, by_place(lane32 & 3, LA), 0.0)
    u = [u_v[f].reshape(32, 128) for f in range(5)]

    wall = [jnp.sum(x * wall_a, axis=1, keepdims=True) for x in u]
    own[...] = jnp.sum(pressure_of(wall) * load_w, axis=0, keepdims=True)

    by_column = jnp.where(first_column & (ax != EXTRA), 2, 1)
    greeted = jnp.where(greets_above, 0, 1) + jnp.where(greets_below, 0, 1)
    greeted = greeted + jnp.where(on_odd_core, 0, jnp.where(ax > 0, 2, 1))
    greeted = greeted + jnp.where(
        ra == 1, 2, jnp.where(ax == ROOT, AZIM, jnp.where(ax >= 4, AZIM + 1, by_column))
    )
    pl.semaphore_wait(barrier, greeted)

    def push(src, dst, lane_of, device):
        return pltpu.make_async_remote_copy(
            src_ref=src,
            dst_ref=dst,
            send_sem=send_sem.at[lane_of],
            recv_sem=recv_sem.at[lane_of],
            device_id=device,
            device_id_type=MESH,
        )

    def arrived(ref, lane_of):
        pltpu.make_async_copy(ref, ref, recv_sem.at[lane_of]).wait()

    def left(ref, lane_of):
        pltpu.make_async_copy(ref, ref, send_sem.at[lane_of]).wait()

    def tell_all(src, dst, lane_of, first):
        def send(i, carry):
            push(src, dst, lane_of, {"azim": lax.rem(az + i, AZIM), "axial": ROOT, "radial": 0}).start()
            return carry

        def send_direct(i, carry):
            push(src, dst, lane_of, {"azim": i, "axial": ROOT, "radial": 0}).start()
            return carry

        if first:
            push(src, dst, lane_of, extra).start()
            lax.fori_loop(1, AZIM, send, 0)
        else:
            send_direct(0, 0)
            push(src, dst, lane_of, extra).start()
            lax.fori_loop(1, AZIM, send_direct, 0)

    @pl.when(is_far & (ax >= 6))
    def _():
        tell_all(own, p2a.at[az * 2 + (ax - 6)], 1, False)

    @pl.when(is_far & (ax < 6))
    def _():
        tell_all(own, p2b.at[az * 2 + (ax - 4)], 8, False)

    @pl.when(is_near)
    def _():
        push(own, p1.at[jnp.where(ax == 0, 0, ax - 1)], 0, column_root).start()

    is_told = jnp.logical_not(is_root | is_extra)

    @pl.when(is_told)
    def _():
        pl.semaphore_signal(ready_sem, inc=1, device_id=column_teller, device_id_type=MESH)

    rho = u[0]
    p = pressure_of(u)
    sound = jnp.sqrt(1.4 * p / rho)
    cos32 = jnp.concatenate([jnp.full((8, 128), cos[a], F32) for a in range(4)], axis=0)
    sin32 = jnp.concatenate([jnp.full((8, 128), sin[a], F32) for a in range(4)], axis=0)
    speed_r = jnp.abs((u[1] * cos32 + u[2] * sin32) / rho) + sound
    speed_a = jnp.abs((u[2] * cos32 - u[1] * sin32) / rho) + sound
    speed_z = jnp.abs(u[3] / rho) + sound

    def rows(x):
        return [x[8 * a : 8 * a + 8] for a in range(4)]

    u_rows = [rows(x) for x in u]
    mean_a = weighed(Q / 2, rows(speed_a))
    for f in range(5):
        azs_lo[f] = weighed(LA, u_rows[f])
        azs_hi[f] = weighed(LB, u_rows[f])
    azs_lo[5] = mean_a
    azs_hi[5] = mean_a

    def push_below():
        push(azs_lo, azr_hi, 3, {"azim": below}).start()

    def push_above():
        push(azs_hi, azr_lo, 4, {"azim": above}).start()

    pl.when(jnp.logical_not(greets_below))(push_below)
    pl.when(jnp.logical_not(greets_above))(push_above)

    loads[5].wait()
    loads[6].wait()
    u_wide = jnp.concatenate(u, axis=1)
    ax_tr = dot(axm[0:72], u_wide)
    ax_sp = dot(axm[72:144], speed_z)
    for f in range(5):
        axs[f] = ax_tr[64:72, 128 * f : 128 * (f + 1)]
    axs[5] = ax_sp[64:72]

    def push_axial_down():
        push(axs, axr_hi, 5, {"axial": ax - 1}).start()

    def push_axial_up():
        push(axs, axr_lo, 6, {"axial": ax + 1}).start()

    pl.when(jnp.logical_not(on_odd_core) & (ax > 0))(push_axial_down)
    pl.when(jnp.logical_not(on_odd_core))(push_axial_up)

    rad_tr = dot(jnp.concatenate(u, axis=0), radm[:, 0:256])
    rad_sp = dot(speed_r, radm[:, 256:512])
    rad_lo = [rad_tr[32 * f : 32 * f + 32, 0:128] for f in range(5)] + [rad_sp[:, 0:128]]
    rad_up = [rad_tr[32 * f : 32 * f + 32, 128:256] for f in range(5)] + [rad_sp[:, 128:256]]
    inner = jnp.full((32, 128), ra, jnp.int32) == 0
    packed = jnp.zeros((32, 128), F32)
    for f in range(6):
        edge = jnp.where(
            inner,
            jnp.broadcast_to(rad_up[f][:, 127:128], (32, 128)),
            jnp.broadcast_to(rad_lo[f][:, 0:1], (32, 128)),
        )
        packed = jnp.where(lane32 == f, edge, packed)
    rads[...] = packed

    @pl.when(ra == 1)
    def _():
        push(rads, radr, 7, {"radial": 0}).start()

    @pl.when(is_root)
    def _():
        arrived(p1, 0)
        col[...] = own[...] + jnp.sum(p1[...], axis=0)
        p2b[2 * AZIM + az] = col[...]
        tell_all(col, p2b.at[2 * AZIM + az], 8, True)

    @pl.when(greets_below)
    def _():
        arrived(azr_lo, 4)
        push_below()

    @pl.when(greets_above)
    def _():
        arrived(azr_hi, 3)
        push_above()

    r32 = jnp.concatenate([r] * 4, axis=0)
    rf32 = jnp.concatenate([r_face] * 4, axis=0)
    k_r = (DT * 2.0 / STEP_R) / r32
    k_a = (DT * 2.0 / STEP_A) / r
    k_a32 = jnp.concatenate([k_a] * 4, axis=0)
    k_z = DT * 2.0 / STEP_Z
    flux_r = still_flux(u, (cos32, sin32))
    flux_a = still_flux(u, (-sin32, cos32))
    flux_z = still_flux(u, None)
    mix_r = dot(
        jnp.concatenate([r32 * x for x in flux_r] + [r32 * x for x in u], axis=0), radm[:, 512:640]
    )
    mix_z = dot(axm[144:176], jnp.concatenate(flux_z + u, axis=1))
    for f in range(5):
        flux_rows = rows(flux_a[f])
        mix_a = jnp.concatenate([weighed(MIX[a], flux_rows) for a in range(4)], axis=0)
        r0[f] = (
            -k_r * mix_r[32 * f : 32 * f + 32]
            - k_a32 * mix_a
            - k_z * mix_z[:, 128 * f : 128 * f + 128]
        )
        br[f] = k_r * mix_r[160 + 32 * f : 192 + 32 * f]
        bz[f] = k_z * mix_z[:, 640 + 128 * f : 768 + 128 * f]

    @pl.when(jnp.logical_not(greets_below))
    def _():
        arrived(azr_lo, 4)

    @pl.when(jnp.logical_not(greets_above))
    def _():
        arrived(azr_hi, 3)

    own_lo = [azs_lo[f] for f in range(6)]
    own_hi = [azs_hi[f] for f in range(6)]
    from_lo = [azr_lo[f] for f in range(6)]
    from_hi = [azr_hi[f] for f in range(6)]
    lo_terms = face_terms(
        from_lo[:5], own_lo[:5], jnp.maximum(from_lo[5], own_lo[5]), (-sin[4], cos[4])
    )
    hi_terms = face_terms(
        own_hi[:5], from_hi[:5], jnp.maximum(from_hi[5], own_hi[5]), (-sin[5], cos[5])
    )
    for f in range(5):
        for a in range(4):
            fix = float(SC[a]) * lo_terms[0][f] + float(SE[a]) * hi_terms[0][f]
            r0[f, 8 * a : 8 * a + 8] = r0[f, 8 * a : 8 * a + 8] - k_a * fix
        aface[f] = k_a * lo_terms[1][f]
        aface[5 + f] = k_a * lo_terms[2][f]
        aface[10 + f] = k_a * hi_terms[1][f]
        aface[15 + f] = k_a * hi_terms[2][f]

    @pl.when(ax > 0)
    def _():
        arrived(axr_lo, 6)
        pl.when(on_odd_core)(push_axial_down)

    @pl.when(ax == 0)
    def _():
        for f in range(6):
            axr_lo[f] = jnp.full((8, 128), (*FREE, 1.5)[f], F32)

    @pl.when(ax < AXIAL - 1)
    def _():
        arrived(axr_hi, 5)
        pl.when(on_odd_core)(push_axial_up)

    @pl.when(ax == AXIAL - 1)
    def _():
        for f in range(6):
            axr_hi[f] = jnp.full((8, 128), (*FREE, 1.5)[f], F32)

    def spread(ref, f, first):
        got = ref[f]
        return jnp.concatenate(
            [jnp.broadcast_to(got[first + a : first + a + 1], (8, 128)) for a in range(4)], axis=0
        )

    minus, plus = [], []
    for f in range(6):
        if f < 5:
            low, up = (ax_tr[32 * i : 32 * i + 32, 128 * f : 128 * f + 128] for i in range(2))
        else:
            low, up = ax_sp[0:32], ax_sp[32:64]
        minus.append(jnp.where(sub32 < 3, spread(axr_lo, f, 4), up))
        plus.append(jnp.where(sub32 == 3, spread(axr_hi, f, 0), low))
    terms = face_terms(minus[:5], plus[:5], jnp.maximum(minus[5], plus[5]), None)
    fix_z = dot(axm[176:208], jnp.concatenate(terms[0] + terms[1] + terms[2], axis=1))
    for f in range(5):
        r0[f] = r0[f] - k_z * fix_z[:, 128 * f : 128 * f + 128]
        bz[f] = bz[f] + k_z * fix_z[:, 640 + 128 * f : 768 + 128 * f]
        cz[f] = k_z * fix_z[:, 1280 + 128 * f : 1408 + 128 * f]

    arrived(radr, 7)

    @pl.when(ra == 0)
    def _():
        push(rads, radr, 7, {"radial": 1}).start()

    lowest = lane32 < 4
    highest = lane32 == 127
    minus, plus = [], []
    got = radr[...]
    for f in range(6):
        ghost = jnp.broadcast_to(got[:, f : f + 1], (32, 128))
        minus.append(jnp.where(lowest, jnp.where(inner, rad_lo[f], ghost), rad_up[f]))
        free = (*FREE, 1.0)[f]
        plus.append(jnp.where(highest, jnp.where(inner, ghost, free), rad_lo[f]))
    base, mean, half_jump = face_terms(
        minus[:5], plus[:5], jnp.maximum(minus[5], plus[5]), (cos32, sin32)
    )
    at_wall = lowest & inner
    pw = pressure_of(plus[:5])
    wall_base = [0.0, pw * cos32, pw * sin32, 0.0, 0.0]
    wall_mean = [0.0, 0.0, 0.0, 0.0, -pw]
    base = [rf32 * jnp.where(at_wall, w, x) for w, x in zip(wall_base, base)]
    mean = [rf32 * jnp.where(at_wall, w, x) for w, x in zip(wall_mean, mean)]
    half_jump = [rf32 * jnp.where(at_wall, 0.0, x) for x in half_jump]
    fix_r = dot(jnp.concatenate(base + mean + half_jump, axis=0), radm[:, 640:768])
    for f in range(5):
        r0[f] = r0[f] - k_r * fix_r[32 * f : 32 * f + 32]
        br[f] = br[f] + k_r * fix_r[160 + 32 * f : 192 + 32 * f]
        cr[f] = k_r * fix_r[320 + 32 * f : 352 + 32 * f]

    @pl.when(is_root)
    def _():
        left(p2b.at[pl.ds(0, AZIM)], 8)

    @pl.when(is_far & (ax >= 6))
    def _():
        left(p2b.at[pl.ds(0, AZIM + 1)], 1)

    @pl.when(is_far & (ax < 6))
    def _():
        left(p2b.at[pl.ds(0, AZIM + 1)], 8)

    @pl.when(is_near)
    def _():
        left(own, 0)

    left(azs_lo, 3)
    left(azs_hi, 4)

    @pl.when(ax > 0)
    def _():
        left(axs, 5)

    @pl.when(ax < AXIAL - 1)
    def _():
        left(axs, 6)

    left(rads, 7)

    loads[7].wait()
    v = [body_s[0, i] for i in range(3)]
    om = [body_s[0, 3 + i] for i in range(3)]
    spin = [om[0], om[1], 0.25 * om[2]]
    gyro = [
        om[1] * spin[2] - om[2] * spin[1],
        om[2] * spin[0] - om[0] * spin[2],
        om[0] * spin[1] - om[1] * spin[0],
    ]


    @pl.when(is_root)
    def _():
        arrived(p2b.at[pl.ds(0, 3 * AZIM - 1)], 8)

    @pl.when(is_extra)
    def _():
        arrived(p2b, 8)

    @pl.when(is_extra)
    def _():
        pl.semaphore_wait(ready_sem, 2 * AXIAL - 2)

    @pl.when(is_teller & is_root)
    def _():
        pl.semaphore_wait(ready_sem, 2 * AXIAL - 1)

    def sum_rows(ref, count):
        sums = [ref[i] for i in range(8)]
        for i in range(8, count):
            sums[i % 8] = sums[i % 8] + ref[i]
        while len(sums) > 1:
            sums = [x + y for x, y in zip(sums[0::2], sums[1::2])]
        return sums[0]

    @pl.when(is_root | is_extra)
    def _():
        early = sum_rows(p2b, 3 * AZIM)
        arrived(p2a, 1)
        p3[...] = early + sum_rows(p2a, 2 * AZIM)

    @pl.when(is_teller)
    def _():
        @pl.when(is_root)
        def _():
            push(p3, p3, 2, {"axial": EXTRA}).start()

        for k in (2, 0, 4, 5, 6, 7):
            push(p3, p3, 2, {"axial": k}).start()
        for k in range(AXIAL):
            push(p3, p3, 2, {"axial": k, "radial": 1}).start()

    @pl.when(is_told)
    def _():
        arrived(p3, 2)

    total = p3[...]
    load = [jnp.broadcast_to(total[:, i : i + 1], (8, 128)) for i in range(4)]
    v0 = v[0] + 60.0 * load[0]
    v1 = v[1] + 60.0 * load[1]
    v2 = jnp.full((8, 128), v[2], F32)
    o0 = om[0] + 30.0 * (load[2] - gyro[0])
    o1 = om[1] + 30.0 * (load[3] - gyro[1])
    o2 = jnp.full((8, 128), om[2] - 120.0 * gyro[2], F32)
    body_row = zero
    for i, value in enumerate((v0, v1, v2, o0, o1, o2)):
        body_row = jnp.where(lane == i, value, body_row)
    body_ref[...] = body_row[0:1, 0:6]

    along_x = v0 + z * o1
    along_y = v1 - z * o0
    swirl = o2 * r

    def azim_speed(k):
        return cos[k] * along_y - sin[k] * along_x + swirl

    s_a = [azim_speed(k) for k in range(4)]
    s_lo, s_hi = azim_speed(4), azim_speed(5)
    s_r = [cos[a] * along_x + sin[a] * along_y for a in range(4)]
    s_z = [v2 + r * (o0 * sin[a] - o1 * cos[a]) for a in range(4)]
    d0, d1, d2 = DT * o0, DT * o1, DT * o2
    for f in range(5):
        carried = [k_a * s_a[k] * u_v[f, k] for k in range(4)]
        at_lo = s_lo * aface[f] + jnp.abs(s_lo) * aface[5 + f]
        at_hi = s_hi * aface[10 + f] + jnp.abs(s_hi) * aface[15 + f]
        for a in range(4):
            row = slice(8 * a, 8 * a + 8)
            value = r0[f, row] + s_r[a] * br[f, row] + jnp.abs(s_r[a]) * cr[f, row]
            value = value + s_z[a] * bz[f, row] + jnp.abs(s_z[a]) * cz[f, row]
            value = value + weighed(MIX[a], carried)
            value = value + float(SC[a]) * at_lo + float(SE[a]) * at_hi
            if f == 1:
                value = value - (d1 * u_v[3, a] - d2 * u_v[2, a])
            if f == 2:
                value = value - (d2 * u_v[1, a] - d0 * u_v[3, a])
            if f == 3:
                value = value - (d0 * u_v[2, a] - d1 * u_v[1, a])
            out_ref[f, a] = value

    @pl.when(is_teller & is_root)
    def _():
        left(p2b.at[pl.ds(0, 2 * AXIAL - 1)], 2)

    @pl.when(is_extra)
    def _():
        left(p2b.at[pl.ds(0, 2 * AXIAL - 2)], 2)


def store_kernel(out_ref, body_ref, rho_h, mom_h, ene_h, body_h, sems):
    copies = [
        pltpu.make_async_copy(src, dst, sems.at[i])
        for i, (src, dst) in enumerate(
            [
                (out_ref.at[pl.ds(1, 3)], mom_h),
                (out_ref.at[0], rho_h),
                (out_ref.at[4], ene_h),
                (body_ref, body_h),
            ]
        )
    ]
    for copy in copies:
        copy.start()
    for copy in copies:
        copy.wait()


def on_device(density, momentum, energy, wall_flags, body_motion):
    block = density.shape
    hbm = pl.BlockSpec(memory_space=pl.ANY)
    vmem = pl.BlockSpec(memory_space=pltpu.VMEM)
    halo = pltpu.VMEM((6, 8, 128), F32)
    part = pltpu.VMEM((5, 32, 128), F32)
    increment, body_row = pl.pallas_call(
        section_kernel,
        out_shape=(pltpu.VMEM((5, *block), F32), pltpu.VMEM((1, 6), F32)),
        in_specs=[hbm] * 8,
        out_specs=(vmem, vmem),
        scratch_shapes=[
            pltpu.VMEM((5, *block), F32),
            pltpu.VMEM((128, 768), F32),
            pltpu.VMEM((208, 32), F32),
            pltpu.SMEM((1, 128), F32),
            pltpu.SMEM((1, 2), jnp.int32),
            pltpu.SMEM((1, 6), F32),
            pltpu.VMEM((1, 128), F32),
            pltpu.VMEM((1, 128), F32),
            pltpu.VMEM((3, 1, 128), F32),
            pltpu.VMEM((2 * AZIM, 1, 128), F32),
            pltpu.VMEM((3 * AZIM, 1, 128), F32),
            pltpu.VMEM((1, 128), F32),
            *[halo] * 7,
            pltpu.VMEM((32, 128), F32),
            pltpu.VMEM((32, 128), F32),
            *[part] * 5,
            pltpu.VMEM((20, 8, 128), F32),
            pltpu.SemaphoreType.DMA((8,)),
            pltpu.SemaphoreType.DMA((9,)),
            pltpu.SemaphoreType.DMA((9,)),
            pltpu.SemaphoreType.REGULAR,
        ],
        compiler_params=pltpu.CompilerParams(
            collective_id=0, has_side_effects=True
        ),
    )(
        density,
        momentum,
        energy,
        wall_flags,
        body_motion.reshape(1, 6),
        jnp.asarray(radial_matrices()),
        jnp.asarray(axial_matrices()),
        jnp.asarray(angle_table()),
    )
    increment = pltpu.with_memory_space_constraint(increment, pltpu.VMEM)
    body_row = pltpu.with_memory_space_constraint(body_row, pltpu.VMEM)
    rho, mom, ene, body = pl.pallas_call(
        store_kernel,
        out_shape=(
            jax.ShapeDtypeStruct(block, F32),
            jax.ShapeDtypeStruct((3, *block), F32),
            jax.ShapeDtypeStruct(block, F32),
            jax.ShapeDtypeStruct((1, 6), F32),
        ),
        in_specs=[vmem, vmem],
        out_specs=[hbm] * 4,
        scratch_shapes=[pltpu.SemaphoreType.DMA((4,))],
    )(increment, body_row)
    return rho, mom, ene, body.reshape(6)


def solution(mesh):
    return jax.shard_map(
        on_device,
        mesh=mesh,
        in_specs=(
            P("azim", "axial", "radial"),
            P(None, "azim", "axial", "radial"),
            P("azim", "axial", "radial"),
            P("azim", "axial"),
            P(),
        ),
        out_specs=(
            P("azim", "axial", "radial"),
            P(None, "azim", "axial", "radial"),
            P("azim", "axial", "radial"),
            P(),
        ),
        check_vma=False,
    )
```

```python
import math

import jax
import jax.numpy as jnp
import numpy as np
from jax import lax
from jax.experimental import pallas as pl
from jax.experimental.pallas import tpu as pltpu
from jax.sharding import PartitionSpec as P

MESH = pl.DeviceIdType.MESH
F32 = jnp.float32

AZIM, AXIAL, RADIAL = 32, 8, 2
ROOT = 1
EXTRA = 3
STEP_A = 2.0 * math.pi / 32
STEP_Z = 8.0 / 16
STEP_R = 2.0 / 64
DT = 0.05 * min(STEP_R, STEP_Z, STEP_A)
FREE = (1.0, 0.0, 0.0, 0.5, 1.0 / (1.4 * 0.4) + 0.125)


def fr_tables():
    outer_point = np.sqrt(3.0 / 7.0 + 2.0 / 7.0 * np.sqrt(6.0 / 5.0))
    inner_point = np.sqrt(3.0 / 7.0 - 2.0 / 7.0 * np.sqrt(6.0 / 5.0))
    points = np.array([-outer_point, -inner_point, inner_point, outer_point])
    outer_weight = (18.0 - np.sqrt(30.0)) / 36.0
    inner_weight = (18.0 + np.sqrt(30.0)) / 36.0
    weights = np.array([outer_weight, inner_weight, inner_weight, outer_weight])
    bary_weights = np.array(
        [1.0 / np.prod([points[i] - points[j] for j in range(4) if j != i]) for i in range(4)]
    )
    derivative = np.zeros((4, 4))
    for i in range(4):
        for j in range(4):
            if i != j:
                derivative[i, j] = bary_weights[j] / bary_weights[i] / (points[i] - points[j])
        derivative[i, i] = -np.sum(derivative[i])

    def basis_at(location):
        return np.array(
            [
                np.prod(
                    [(location - points[j]) / (points[i] - points[j]) for j in range(4) if j != i]
                )
                for i in range(4)
            ]
        )

    at_lower = basis_at(-1.0)
    at_upper = basis_at(1.0)
    third_slope = 0.5 * (15.0 * points * points - 3.0)
    fourth_slope = 0.5 * (35.0 * points**3 - 15.0 * points)
    slope_left = 0.5 * (fourth_slope - third_slope)
    slope_right = 0.5 * (fourth_slope + third_slope)
    return (points, weights, derivative, at_lower, at_upper, slope_left, slope_right)


X, Q, D, LA, LB, SC, SE = fr_tables()
OFF = (X + 1.0) / 2.0
MIX = D - np.outer(SC, LA) - np.outer(SE, LB)


def radial_matrices():
    low, up, mean_own, mean_below, mix, corr = (np.zeros((128, 128)) for _ in range(6))
    for j in range(128):
        e, k = divmod(j, 4)
        below = 31 if j == 127 else e - 1
        for i in range(4):
            low[4 * e + i, j] = LA[i]
            mean_own[4 * e + i, j] = Q[i] / 2
            mix[4 * e + i, j] = MIX[k, i]
            if below >= 0:
                up[4 * below + i, j] = LB[i]
                mean_below[4 * below + i, j] = Q[i] / 2
        corr[4 * e, j] += SC[k]
        corr[127 if e == 31 else 4 * (e + 1), j] += SE[k]
    return np.concatenate([low, up, mean_own, mean_below, mix, corr], axis=1).astype(np.float32)


def axial_matrices():
    low, up, mean_low, mean_up, mix, corr = (np.zeros((8, 8)) for _ in range(6))
    for j in range(8):
        e, k = divmod(j, 4)
        own = None if j == 3 else e
        below = 1 if j == 3 else (0 if e == 1 else None)
        for i in range(4):
            if own is not None:
                low[j, 4 * own + i] = LA[i]
                mean_low[j, 4 * own + i] = Q[i] / 2
            if below is not None:
                up[j, 4 * below + i] = LB[i]
                mean_up[j, 4 * below + i] = Q[i] / 2
            mix[j, 4 * e + i] = MIX[k, i]
        corr[j, 4 * e] += SC[k]
        corr[j, 4 if e == 0 else 3] += SE[k]
    pack, pack_mean = np.zeros((8, 32)), np.zeros((8, 32))
    for a in range(4):
        for i in range(4):
            pack[a, 8 * a + i] = LA[i]
            pack[4 + a, 8 * a + 4 + i] = LB[i]
            pack_mean[a, 8 * a + i] = Q[i] / 2
            pack_mean[4 + a, 8 * a + 4 + i] = Q[i] / 2
    four = np.eye(4)
    parts = [np.kron(four, low), np.kron(four, up), pack]
    parts += [np.kron(four, mean_low), np.kron(four, mean_up), pack_mean]
    parts += [np.kron(four, mix), np.kron(four, corr)]
    return np.concatenate(parts, axis=0).astype(np.float32)


def angle_table():
    table = np.zeros((32, 128))
    for e in range(32):
        angles = np.array([*(e + OFF), e, e + 1.0]) * STEP_A
        table[e, 0:6] = np.cos(angles)
        table[e, 6:12] = np.sin(angles)
    return table.astype(np.float32)


def dot(a, b):
    return jnp.dot(a, b, precision=lax.Precision.HIGHEST, preferred_element_type=F32)


def weighed(factors, values):
    total = float(factors[0]) * values[0]
    for factor, value in zip(factors[1:], values[1:]):
        total = total + float(factor) * value
    return total


def pressure_of(u):
    return 0.4 * (u[4] - 0.5 * (u[1] * u[1] + u[2] * u[2] + u[3] * u[3]) / u[0])


def still_flux(u, normal):
    p = pressure_of(u)
    through = u[3] if normal is None else u[1] * normal[0] + u[2] * normal[1]
    vn = through / u[0]
    flux = [through, u[1] * vn, u[2] * vn, u[3] * vn, (u[4] + p) * vn]
    if normal is None:
        flux[3] = flux[3] + p
    else:
        flux[1] = flux[1] + p * normal[0]
        flux[2] = flux[2] + p * normal[1]
    return flux


def face_terms(minus, plus, bound, normal):
    low, high = still_flux(minus, normal), still_flux(plus, normal)
    half_jump = [0.5 * (b - a) for a, b in zip(minus, plus)]
    mean = [0.5 * (a + b) for a, b in zip(minus, plus)]
    base = [0.5 * (a + b) - bound * h for a, b, h in zip(low, high, half_jump)]
    return base, mean, half_jump


def section_kernel(
    rho_h, mom_h, ene_h, flag_h, body_h, radm_h, axm_h, ang_h,
    out_ref, body_ref,
    u_v, radm, axm, ang_s, flag_s, body_s,
    own, col, p1, p2a, p2b, p3,
    azs_lo, azs_hi, azr_lo, azr_hi, axs, axr_lo, axr_hi, rads, radr,
    r0, br, cr, bz, cz, by, bo, aface,
    load_sem, send_sem, recv_sem, ready_sem,
):
    az, ax, ra = lax.axis_index("azim"), lax.axis_index("axial"), lax.axis_index("radial")
    is_root = (ra == 0) & (ax == ROOT)
    is_near = (ra == 0) & (ax < 4) & (ax != ROOT)
    first_column = az == 0
    is_extra = first_column & (ra == 0) & (ax == EXTRA)
    is_teller = is_extra | (is_root & jnp.logical_not(first_column))
    is_far = (ra == 0) & (ax >= 4)
    is_even = lax.rem(az, 2) == 0
    late = (ax == 0) & (ra == 0)
    greets_above = (is_even & jnp.logical_not(late & (az == 0))) | (late & (az == AZIM - 1))
    greets_below = (is_even & jnp.logical_not(late & (az == 0))) | (late & (az == 1))
    on_odd_core = lax.rem(ax, 2) == 1
    column_root = {"axial": ROOT, "radial": 0}
    column_teller = {"axial": jnp.where(first_column, EXTRA, ROOT), "radial": 0}
    extra = {"azim": 0, "axial": EXTRA, "radial": 0}

    loads = [
        pltpu.make_async_copy(src, dst, load_sem.at[i])
        for i, (src, dst) in enumerate(
            [
                (ang_h.at[pl.ds(az, 1)], ang_s),
                (flag_h, flag_s),
                (rho_h, u_v.at[0]),
                (mom_h, u_v.at[pl.ds(1, 3)]),
                (ene_h, u_v.at[4]),
                (radm_h, radm),
                (axm_h, axm),
                (body_h, body_s),
            ]
        )
    ]
    for load in loads:
        load.start()

    barrier = pltpu.get_barrier_semaphore()

    def greet(device):
        pl.semaphore_signal(barrier, inc=1, device_id=device, device_id_type=MESH)

    @pl.when(is_root | is_extra)
    def _():
        def greet_column(i, carry):
            for k in (7, 6, 5, 4):
                greet({"azim": i, "axial": k, "radial": 0})
            return carry

        lax.fori_loop(0, AZIM, greet_column, 0)

    @pl.when(is_root)
    def _():
        def greet_root(i, carry):
            greet({"azim": lax.rem(az + i, AZIM)})
            return carry

        lax.fori_loop(1, AZIM, greet_root, 0)
        for k in (0, 2, 3):
            greet({"axial": k})

    @pl.when(is_extra)
    def _():
        def greet_root(i, carry):
            greet({"azim": i, "axial": ROOT})
            return carry

        lax.fori_loop(0, AZIM, greet_root, 0)
        for k in (0, 2):
            greet({"axial": k})

    @pl.when(is_teller)
    def _():
        for k in range(AXIAL):
            greet({"axial": k, "radial": 1})

    below = lax.rem(az + (AZIM - 1), AZIM)
    above = lax.rem(az + 1, AZIM)
    @pl.when(greets_above)
    def _():
        greet({"azim": above})

    @pl.when(greets_below)
    def _():
        greet({"azim": below})

    @pl.when(on_odd_core)
    def _():
        greet({"axial": ax - 1})

    @pl.when(on_odd_core & (ax < AXIAL - 1))
    def _():
        greet({"axial": ax + 1})

    @pl.when(ra == 0)
    def _():
        greet({"radial": 1})

    sub = lax.broadcasted_iota(jnp.int32, (8, 128), 0)
    lane = lax.broadcasted_iota(jnp.int32, (8, 128), 1)
    lane32 = lax.broadcasted_iota(jnp.int32, (32, 128), 1)
    sub32 = lax.broadcasted_iota(jnp.int32, (32, 128), 0) & 7

    def by_place(place, values):
        out = jnp.full(place.shape, float(values[3]), F32)
        for k in range(3):
            out = jnp.where(place == k, float(values[k]), out)
        return out

    z = ((ax * 2 + (sub >> 2)).astype(F32) + by_place(sub & 3, OFF)) * STEP_Z
    elem_r = (ra * 32 + (lane >> 2)).astype(F32)
    r = 1.0 + (elem_r + by_place(lane & 3, OFF)) * STEP_R
    r_face = 1.0 + (elem_r + jnp.where(lane == 127, 1.0, 0.0)) * STEP_R

    for load in loads[:5]:
        load.wait()
    cos = [ang_s[0, k] for k in range(6)]
    sin = [ang_s[0, 6 + k] for k in range(6)]
    flag = jnp.where(
        sub < 4,
        jnp.full((8, 128), flag_s[0, 0], jnp.int32),
        jnp.full((8, 128), flag_s[0, 1], jnp.int32),
    ).astype(F32)
    area_z = flag * by_place(sub & 3, Q * (0.5 * STEP_Z))
    zero = jnp.zeros((8, 128), F32)
    load_w = []
    for a in range(4):
        arm = jnp.where(lane >= 2, z, 1.0) * area_z * float(Q[a] * (0.5 * STEP_A))
        turn = jnp.where((lane == 0) | (lane == 3), -cos[a], jnp.where(lane == 1, -sin[a], sin[a]))
        load_w.append(jnp.where(lane < 4, arm * turn, zero))
    load_w = jnp.concatenate(load_w, axis=0)
    wall_a = jnp.where(lane32 < 4, by_place(lane32 & 3, LA), 0.0)
    u = [u_v[f].reshape(32, 128) for f in range(5)]

    wall = [jnp.sum(x * wall_a, axis=1, keepdims=True) for x in u]
    own[...] = jnp.sum(pressure_of(wall) * load_w, axis=0, keepdims=True)

    by_column = jnp.where(first_column & (ax != EXTRA), 2, 1)
    greeted = jnp.where(greets_above, 0, 1) + jnp.where(greets_below, 0, 1)
    greeted = greeted + jnp.where(on_odd_core, 0, jnp.where(ax > 0, 2, 1))
    greeted = greeted + jnp.where(
        ra == 1, 2, jnp.where(ax == ROOT, AZIM, jnp.where(ax >= 4, AZIM + 1, by_column))
    )
    pl.semaphore_wait(barrier, greeted)

    def push(src, dst, lane_of, device):
        return pltpu.make_async_remote_copy(
            src_ref=src,
            dst_ref=dst,
            send_sem=send_sem.at[lane_of],
            recv_sem=recv_sem.at[lane_of],
            device_id=device,
            device_id_type=MESH,
        )

    def arrived(ref, lane_of):
        pltpu.make_async_copy(ref, ref, recv_sem.at[lane_of]).wait()

    def left(ref, lane_of):
        pltpu.make_async_copy(ref, ref, send_sem.at[lane_of]).wait()

    def tell_all(src, dst, lane_of, first):
        def send(i, carry):
            push(src, dst, lane_of, {"azim": lax.rem(az + i, AZIM), "axial": ROOT, "radial": 0}).start()
            return carry

        def send_direct(i, carry):
            push(src, dst, lane_of, {"azim": i, "axial": ROOT, "radial": 0}).start()
            return carry

        if first:
            push(src, dst, lane_of, extra).start()
            lax.fori_loop(1, AZIM, send, 0)
        else:
            send_direct(0, 0)
            push(src, dst, lane_of, extra).start()
            lax.fori_loop(1, AZIM, send_direct, 0)

    @pl.when(is_far & (ax >= 6))
    def _():
        tell_all(own, p2a.at[az * 2 + (ax - 6)], 1, False)

    @pl.when(is_far & (ax < 6))
    def _():
        tell_all(own, p2b.at[az * 2 + (ax - 4)], 8, False)

    @pl.when(is_near)
    def _():
        push(own, p1.at[jnp.where(ax == 0, 0, ax - 1)], 0, column_root).start()

    is_told = jnp.logical_not(is_root | is_extra)

    @pl.when(is_told)
    def _():
        pl.semaphore_signal(ready_sem, inc=1, device_id=column_teller, device_id_type=MESH)

    rho = u[0]
    p = pressure_of(u)
    sound = jnp.sqrt(1.4 * p / rho)
    cos32 = jnp.concatenate([jnp.full((8, 128), cos[a], F32) for a in range(4)], axis=0)
    sin32 = jnp.concatenate([jnp.full((8, 128), sin[a], F32) for a in range(4)], axis=0)
    speed_r = jnp.abs((u[1] * cos32 + u[2] * sin32) / rho) + sound
    speed_a = jnp.abs((u[2] * cos32 - u[1] * sin32) / rho) + sound
    speed_z = jnp.abs(u[3] / rho) + sound

    def rows(x):
        return [x[8 * a : 8 * a + 8] for a in range(4)]

    u_rows = [rows(x) for x in u]
    mean_a = weighed(Q / 2, rows(speed_a))
    for f in range(5):
        azs_lo[f] = weighed(LA, u_rows[f])
        azs_hi[f] = weighed(LB, u_rows[f])
    azs_lo[5] = mean_a
    azs_hi[5] = mean_a

    def push_below():
        push(azs_lo, azr_hi, 3, {"azim": below}).start()

    def push_above():
        push(azs_hi, azr_lo, 4, {"azim": above}).start()

    pl.when(jnp.logical_not(greets_below))(push_below)
    pl.when(jnp.logical_not(greets_above))(push_above)

    loads[5].wait()
    loads[6].wait()
    u_wide = jnp.concatenate(u, axis=1)
    ax_tr = dot(axm[0:72], u_wide)
    ax_sp = dot(axm[72:144], speed_z)
    for f in range(5):
        axs[f] = ax_tr[64:72, 128 * f : 128 * (f + 1)]
    axs[5] = ax_sp[64:72]

    def push_axial_down():
        push(axs, axr_hi, 5, {"axial": ax - 1}).start()

    def push_axial_up():
        push(axs, axr_lo, 6, {"axial": ax + 1}).start()

    pl.when(jnp.logical_not(on_odd_core) & (ax > 0))(push_axial_down)
    pl.when(jnp.logical_not(on_odd_core))(push_axial_up)

    rad_tr = dot(jnp.concatenate(u, axis=0), radm[:, 0:256])
    rad_sp = dot(speed_r, radm[:, 256:512])
    rad_lo = [rad_tr[32 * f : 32 * f + 32, 0:128] for f in range(5)] + [rad_sp[:, 0:128]]
    rad_up = [rad_tr[32 * f : 32 * f + 32, 128:256] for f in range(5)] + [rad_sp[:, 128:256]]
    inner = jnp.full((32, 128), ra, jnp.int32) == 0
    packed = jnp.zeros((32, 128), F32)
    for f in range(6):
        edge = jnp.where(
            inner,
            jnp.broadcast_to(rad_up[f][:, 127:128], (32, 128)),
            jnp.broadcast_to(rad_lo[f][:, 0:1], (32, 128)),
        )
        packed = jnp.where(lane32 == f, edge, packed)
    rads[...] = packed

    @pl.when(ra == 1)
    def _():
        push(rads, radr, 7, {"radial": 0}).start()

    @pl.when(is_root)
    def _():
        arrived(p1, 0)
        col[...] = own[...] + jnp.sum(p1[...], axis=0)
        p2b[2 * AZIM + az] = col[...]
        tell_all(col, p2b.at[2 * AZIM + az], 8, True)

    @pl.when(greets_below)
    def _():
        arrived(azr_lo, 4)
        push_below()

    @pl.when(greets_above)
    def _():
        arrived(azr_hi, 3)
        push_above()

    r32 = jnp.concatenate([r] * 4, axis=0)
    rf32 = jnp.concatenate([r_face] * 4, axis=0)
    k_r = (DT * 2.0 / STEP_R) / r32
    k_a = (DT * 2.0 / STEP_A) / r
    k_a32 = jnp.concatenate([k_a] * 4, axis=0)
    k_z = DT * 2.0 / STEP_Z
    flux_r = still_flux(u, (cos32, sin32))
    flux_a = still_flux(u, (-sin32, cos32))
    flux_z = still_flux(u, None)
    mix_r = dot(
        jnp.concatenate([r32 * x for x in flux_r] + [r32 * x for x in u], axis=0), radm[:, 512:640]
    )
    mix_z = dot(axm[144:176], jnp.concatenate(flux_z + u, axis=1))
    for f in range(5):
        flux_rows = rows(flux_a[f])
        mix_a = jnp.concatenate([weighed(MIX[a], flux_rows) for a in range(4)], axis=0)
        r0[f] = (
            -k_r * mix_r[32 * f : 32 * f + 32]
            - k_a32 * mix_a
            - k_z * mix_z[:, 128 * f : 128 * f + 128]
        )
        br[f] = k_r * mix_r[160 + 32 * f : 192 + 32 * f]
        bz[f] = k_z * mix_z[:, 640 + 128 * f : 768 + 128 * f]

    @pl.when(jnp.logical_not(greets_below))
    def _():
        arrived(azr_lo, 4)

    @pl.when(jnp.logical_not(greets_above))
    def _():
        arrived(azr_hi, 3)

    own_lo = [azs_lo[f] for f in range(6)]
    own_hi = [azs_hi[f] for f in range(6)]
    from_lo = [azr_lo[f] for f in range(6)]
    from_hi = [azr_hi[f] for f in range(6)]
    lo_terms = face_terms(
        from_lo[:5], own_lo[:5], jnp.maximum(from_lo[5], own_lo[5]), (-sin[4], cos[4])
    )
    hi_terms = face_terms(
        own_hi[:5], from_hi[:5], jnp.maximum(from_hi[5], own_hi[5]), (-sin[5], cos[5])
    )
    for f in range(5):
        for a in range(4):
            fix = float(SC[a]) * lo_terms[0][f] + float(SE[a]) * hi_terms[0][f]
            r0[f, 8 * a : 8 * a + 8] = r0[f, 8 * a : 8 * a + 8] - k_a * fix
        aface[f] = k_a * lo_terms[1][f]
        aface[5 + f] = k_a * lo_terms[2][f]
        aface[10 + f] = k_a * hi_terms[1][f]
        aface[15 + f] = k_a * hi_terms[2][f]

    @pl.when(ax > 0)
    def _():
        arrived(axr_lo, 6)
        pl.when(on_odd_core)(push_axial_down)

    @pl.when(ax == 0)
    def _():
        for f in range(6):
            axr_lo[f] = jnp.full((8, 128), (*FREE, 1.5)[f], F32)

    @pl.when(ax < AXIAL - 1)
    def _():
        arrived(axr_hi, 5)
        pl.when(on_odd_core)(push_axial_up)

    @pl.when(ax == AXIAL - 1)
    def _():
        for f in range(6):
            axr_hi[f] = jnp.full((8, 128), (*FREE, 1.5)[f], F32)

    def spread(ref, f, first):
        got = ref[f]
        return jnp.concatenate(
            [jnp.broadcast_to(got[first + a : first + a + 1], (8, 128)) for a in range(4)], axis=0
        )

    minus, plus = [], []
    for f in range(6):
        if f < 5:
            low, up = (ax_tr[32 * i : 32 * i + 32, 128 * f : 128 * f + 128] for i in range(2))
        else:
            low, up = ax_sp[0:32], ax_sp[32:64]
        minus.append(jnp.where(sub32 < 3, spread(axr_lo, f, 4), up))
        plus.append(jnp.where(sub32 == 3, spread(axr_hi, f, 0), low))
    terms = face_terms(minus[:5], plus[:5], jnp.maximum(minus[5], plus[5]), None)
    fix_z = dot(axm[176:208], jnp.concatenate(terms[0] + terms[1] + terms[2], axis=1))
    for f in range(5):
        r0[f] = r0[f] - k_z * fix_z[:, 128 * f : 128 * f + 128]
        bz[f] = bz[f] + k_z * fix_z[:, 640 + 128 * f : 768 + 128 * f]
        cz[f] = k_z * fix_z[:, 1280 + 128 * f : 1408 + 128 * f]

    arrived(radr, 7)

    @pl.when(ra == 0)
    def _():
        push(rads, radr, 7, {"radial": 1}).start()

    lowest = lane32 < 4
    highest = lane32 == 127
    minus, plus = [], []
    got = radr[...]
    for f in range(6):
        ghost = jnp.broadcast_to(got[:, f : f + 1], (32, 128))
        minus.append(jnp.where(lowest, jnp.where(inner, rad_lo[f], ghost), rad_up[f]))
        free = (*FREE, 1.0)[f]
        plus.append(jnp.where(highest, jnp.where(inner, ghost, free), rad_lo[f]))
    base, mean, half_jump = face_terms(
        minus[:5], plus[:5], jnp.maximum(minus[5], plus[5]), (cos32, sin32)
    )
    at_wall = lowest & inner
    pw = pressure_of(plus[:5])
    wall_base = [0.0, pw * cos32, pw * sin32, 0.0, 0.0]
    wall_mean = [0.0, 0.0, 0.0, 0.0, -pw]
    base = [rf32 * jnp.where(at_wall, w, x) for w, x in zip(wall_base, base)]
    mean = [rf32 * jnp.where(at_wall, w, x) for w, x in zip(wall_mean, mean)]
    half_jump = [rf32 * jnp.where(at_wall, 0.0, x) for x in half_jump]
    fix_r = dot(jnp.concatenate(base + mean + half_jump, axis=0), radm[:, 640:768])
    for f in range(5):
        r0[f] = r0[f] - k_r * fix_r[32 * f : 32 * f + 32]
        br[f] = br[f] + k_r * fix_r[160 + 32 * f : 192 + 32 * f]
        cr[f] = k_r * fix_r[320 + 32 * f : 352 + 32 * f]

    @pl.when(is_root)
    def _():
        left(p2b.at[pl.ds(0, AZIM)], 8)

    @pl.when(is_far & (ax >= 6))
    def _():
        left(p2b.at[pl.ds(0, AZIM + 1)], 1)

    @pl.when(is_far & (ax < 6))
    def _():
        left(p2b.at[pl.ds(0, AZIM + 1)], 8)

    @pl.when(is_near)
    def _():
        left(own, 0)

    left(azs_lo, 3)
    left(azs_hi, 4)

    @pl.when(ax > 0)
    def _():
        left(axs, 5)

    @pl.when(ax < AXIAL - 1)
    def _():
        left(axs, 6)

    left(rads, 7)

    loads[7].wait()
    v = [body_s[0, i] for i in range(3)]
    om = [body_s[0, 3 + i] for i in range(3)]
    spin = [om[0], om[1], 0.25 * om[2]]
    gyro = [
        om[1] * spin[2] - om[2] * spin[1],
        om[2] * spin[0] - om[0] * spin[2],
        om[0] * spin[1] - om[1] * spin[0],
    ]

    o2 = om[2] - 120.0 * gyro[2]
    swirl = o2 * r
    for f in range(5):
        carried = [k_a * u_v[f, k] for k in range(4)]
        below_mean, above_mean = aface[f], aface[10 + f]
        for a in range(4):
            row = slice(8 * a, 8 * a + 8)
            part = [float(MIX[a, k]) * carried[k] for k in range(4)]
            part += [float(SC[a]) * below_mean, float(SE[a]) * above_mean]
            plain = sum(part[1:], part[0])
            of_x = cos[a] * br[f, row] - sum((sin[k] * part[k] for k in range(1, 6)), sin[0] * part[0])
            of_y = sin[a] * br[f, row] + sum((cos[k] * part[k] for k in range(1, 6)), cos[0] * part[0])
            arm = r * bz[f, row]
            of_o0 = sin[a] * arm - z * of_y
            of_o1 = z * of_x - cos[a] * arm
            value = r0[f, row] + swirl * plain + v[2] * bz[f, row]
            if f == 1:
                value = value + (DT * o2) * u_v[2, a]
                of_o1 = of_o1 - DT * u_v[3, a]
            if f == 2:
                value = value - (DT * o2) * u_v[1, a]
                of_o0 = of_o0 + DT * u_v[3, a]
            if f == 3:
                of_o0 = of_o0 - DT * u_v[2, a]
                of_o1 = of_o1 + DT * u_v[1, a]
            r0[f, row] = value
            br[f, row] = of_x
            by[f, row] = of_y
            bz[f, row] = of_o0
            bo[f, row] = of_o1


    @pl.when(is_root)
    def _():
        arrived(p2b.at[pl.ds(0, 3 * AZIM - 1)], 8)

    @pl.when(is_extra)
    def _():
        arrived(p2b, 8)

    @pl.when(is_extra)
    def _():
        pl.semaphore_wait(ready_sem, 2 * AXIAL - 2)

    @pl.when(is_teller & is_root)
    def _():
        pl.semaphore_wait(ready_sem, 2 * AXIAL - 1)

    def sum_rows(ref, count):
        sums = [ref[i] for i in range(8)]
        for i in range(8, count):
            sums[i % 8] = sums[i % 8] + ref[i]
        while len(sums) > 1:
            sums = [x + y for x, y in zip(sums[0::2], sums[1::2])]
        return sums[0]

    @pl.when(is_root | is_extra)
    def _():
        col[...] = sum_rows(p2b, 3 * AZIM)
        arrived(p2a, 1)
        p3[...] = col[...] + sum_rows(p2a, 2 * AZIM)

    @pl.when(is_teller)
    def _():
        @pl.when(is_root)
        def _():
            push(p3, p3, 2, {"axial": EXTRA}).start()

        for k in (2, 0, 4, 5, 6, 7):
            push(p3, p3, 2, {"axial": k}).start()
        for k in range(AXIAL):
            push(p3, p3, 2, {"axial": k, "radial": 1}).start()

    @pl.when(is_told)
    def _():
        arrived(p3, 2)

    total = p3[...]
    load = [jnp.broadcast_to(total[:, i : i + 1], (8, 128)) for i in range(4)]
    v0 = v[0] + 60.0 * load[0]
    v1 = v[1] + 60.0 * load[1]
    o0 = om[0] + 30.0 * (load[2] - gyro[0])
    o1 = om[1] + 30.0 * (load[3] - gyro[1])
    body_row = zero
    for i, value in enumerate((v0, v1, v[2], o0, o1, o2)):
        body_row = jnp.where(lane == i, value, body_row)
    body_ref[...] = body_row[0:1, 0:6]

    along_x = v0 + z * o1
    along_y = v1 - z * o0

    def azim_speed(k):
        return jnp.abs(cos[k] * along_y - sin[k] * along_x + swirl)

    s_lo, s_hi = azim_speed(4), azim_speed(5)
    s_r = [jnp.abs(cos[a] * along_x + sin[a] * along_y) for a in range(4)]
    s_z = [jnp.abs(v[2] + r * (o0 * sin[a] - o1 * cos[a])) for a in range(4)]
    for f in range(5):
        at_lo, at_hi = s_lo * aface[5 + f], s_hi * aface[15 + f]
        for a in range(4):
            row = slice(8 * a, 8 * a + 8)
            value = (r0[f, row] + v0 * br[f, row]) + (v1 * by[f, row] + o0 * bz[f, row])
            value = value + (o1 * bo[f, row] + s_r[a] * cr[f, row])
            value = value + (s_z[a] * cz[f, row] + float(SC[a]) * at_lo + float(SE[a]) * at_hi)
            out_ref[f, a] = value

    @pl.when(is_teller & is_root)
    def _():
        left(p2b.at[pl.ds(0, 2 * AXIAL - 1)], 2)

    @pl.when(is_extra)
    def _():
        left(p2b.at[pl.ds(0, 2 * AXIAL - 2)], 2)


def store_kernel(out_ref, body_ref, rho_h, mom_h, ene_h, body_h, sems):
    copies = [
        pltpu.make_async_copy(src, dst, sems.at[i])
        for i, (src, dst) in enumerate(
            [
                (out_ref.at[pl.ds(1, 3)], mom_h),
                (out_ref.at[0], rho_h),
                (out_ref.at[4], ene_h),
                (body_ref, body_h),
            ]
        )
    ]
    for copy in copies:
        copy.start()
    for copy in copies:
        copy.wait()


def on_device(density, momentum, energy, wall_flags, body_motion):
    block = density.shape
    hbm = pl.BlockSpec(memory_space=pl.ANY)
    vmem = pl.BlockSpec(memory_space=pltpu.VMEM)
    halo = pltpu.VMEM((6, 8, 128), F32)
    part = pltpu.VMEM((5, 32, 128), F32)
    increment, body_row = pl.pallas_call(
        section_kernel,
        out_shape=(pltpu.VMEM((5, *block), F32), pltpu.VMEM((1, 6), F32)),
        in_specs=[hbm] * 8,
        out_specs=(vmem, vmem),
        scratch_shapes=[
            pltpu.VMEM((5, *block), F32),
            pltpu.VMEM((128, 768), F32),
            pltpu.VMEM((208, 32), F32),
            pltpu.SMEM((1, 128), F32),
            pltpu.SMEM((1, 2), jnp.int32),
            pltpu.SMEM((1, 6), F32),
            pltpu.VMEM((1, 128), F32),
            pltpu.VMEM((1, 128), F32),
            pltpu.VMEM((3, 1, 128), F32),
            pltpu.VMEM((2 * AZIM, 1, 128), F32),
            pltpu.VMEM((3 * AZIM, 1, 128), F32),
            pltpu.VMEM((1, 128), F32),
            *[halo] * 7,
            pltpu.VMEM((32, 128), F32),
            pltpu.VMEM((32, 128), F32),
            *[part] * 7,
            pltpu.VMEM((20, 8, 128), F32),
            pltpu.SemaphoreType.DMA((8,)),
            pltpu.SemaphoreType.DMA((9,)),
            pltpu.SemaphoreType.DMA((9,)),
            pltpu.SemaphoreType.REGULAR,
        ],
        compiler_params=pltpu.CompilerParams(
            collective_id=0, has_side_effects=True
        ),
    )(
        density,
        momentum,
        energy,
        wall_flags,
        body_motion.reshape(1, 6),
        jnp.asarray(radial_matrices()),
        jnp.asarray(axial_matrices()),
        jnp.asarray(angle_table()),
    )
    increment = pltpu.with_memory_space_constraint(increment, pltpu.VMEM)
    body_row = pltpu.with_memory_space_constraint(body_row, pltpu.VMEM)
    rho, mom, ene, body = pl.pallas_call(
        store_kernel,
        out_shape=(
            jax.ShapeDtypeStruct(block, F32),
            jax.ShapeDtypeStruct((3, *block), F32),
            jax.ShapeDtypeStruct(block, F32),
            jax.ShapeDtypeStruct((1, 6), F32),
        ),
        in_specs=[vmem, vmem],
        out_specs=[hbm] * 4,
        scratch_shapes=[pltpu.SemaphoreType.DMA((4,))],
    )(increment, body_row)
    return rho, mom, ene, body.reshape(6)


def solution(mesh):
    return jax.shard_map(
        on_device,
        mesh=mesh,
        in_specs=(
            P("azim", "axial", "radial"),
            P(None, "azim", "axial", "radial"),
            P("azim", "axial", "radial"),
            P("azim", "axial"),
            P(),
        ),
        out_specs=(
            P("azim", "axial", "radial"),
            P(None, "azim", "axial", "radial"),
            P("azim", "axial", "radial"),
            P(),
        ),
        check_vma=False,
    )
```
